256 devices in a mesh: ctx: 128 (over z, y_lo, x, core), head: 2 (over y_hi).
Axes of the slice: x: 4, y: 4 (y_hi: 2, y_lo: 2; y = y_hi * 2 + y_lo), z: 8, core: 2. Of those that a mesh axis runs over, the one named last changes fastest.
Arguments:
- index_queries: bfloat16 [64, 64, 128], P(None, 'head'), may hold values from -310 to 310
- head_weights: float32 [64, 64], P(None, 'head'), may hold values from -4 to 4
- index_keys: bfloat16 [131072, 128], P('ctx'), may hold values from -6 to 6
- main_target: float32 [64, 131072], P(None, 'ctx'), may hold values from 0.01 to 1
Outputs:
- grad_queries: float32 [64, 64, 128], P(None, 'head')
- grad_weights: float32 [64, 64], P(None, 'head')
- grad_keys: float32 [131072, 128], P('ctx')
- loss_rows: float32 [64], replicated
The draws below stay inside these ranges and needn't reach their ends.
All inputs are finite; a program needn't handle non-finite values.
Results may differ from the reference program's by a relative error of at most 0.007.
Values sent between devices are 32-bit elements; how exact they have to be, the bound alone decides.
No kernel may reach another device: no remote copies, remote signals or barrier semaphores. Data moves between devices by JAX's collectives and lax.ppermute only.
A program may use at most 64 MiB of HBM per device.

```python
import math
import jax
import jax.numpy as jnp
from jax import lax

H = 64
DI = 128
QC = 64
KDEV = 1024
KTOT = 131072
N_CTX = 128


def draw_index_queries(key, part):
    key = jax.random.fold_in(key, 11)
    values = jnp.clip(jax.random.normal(key, (QC, H, DI), jnp.float32), -4.0, 4.0)
    return values.astype(jnp.bfloat16)


def steps_of(key, extent, pieces, least, high):
    loudness, own = 1.0, jax.random.fold_in(key, 6)
    for position, shards_of in pieces:
        draws = jnp.exp(jax.random.uniform(jax.random.fold_in(own, position), (shards_of,), jnp.float32, least / len(pieces), high / len(pieces)))
        loudness = loudness * jnp.repeat(draws, extent[position] // shards_of).reshape([-1 if axis == position else 1 for axis in range(len(extent))])
    return loudness


def scatter_about(own_key, extent, deviation, bound, pieces=(), held_as=jnp.bfloat16):
    array = jax.random.normal(own_key, extent, jnp.float32) * deviation
    if len(pieces) > 0:
        array = steps_of(own_key, extent, pieces, -0.22, 0.18) * array
    return jnp.clip(array, min=-bound, max=bound).astype(held_as)


def setup_inputs(seed: int = 0) -> dict:
    seeds = jax.random.split(jax.random.key(seed), 5)
    index_queries = draw_index_queries(jax.random.fold_in(seeds[4], 71), 0)
    head_weights = scatter_about(seeds[1], (QC, H), 1.0, 4.0, ((1, 2),), jnp.float32)
    index_keys = scatter_about(seeds[2], (KTOT, DI), 1.0, 6.0, ((0, 128),))
    main_target = jnp.clip(jnp.exp(math.log(1.0) - 4.6051702 * jax.random.uniform(seeds[3], (QC, KTOT), jnp.float32) ** steps_of(seeds[3], (QC, KTOT), ((1, 128),), -0.2, 0.2)), 0.01, 1.0)
    return dict(index_queries=index_queries, head_weights=head_weights, index_keys=index_keys, main_target=main_target)


def reference(index_queries, head_weights, index_keys, main_target):
    scale_width = DI ** -0.5
    scale_heads = H ** -0.5
    highest = lax.Precision.HIGHEST
    queries_f = index_queries.astype(jnp.float32)
    key_blocks = index_keys.reshape(N_CTX, KDEV, DI)

    def score_block(block):
        logits = jnp.einsum("tjd,sd->tjs", queries_f, block.astype(jnp.float32), precision=highest) * scale_width
        return jnp.einsum("tj,tjs->ts", head_weights, jnp.maximum(logits, 0.0), precision=highest) * scale_heads

    index = lax.map(score_block, key_blocks)
    index = jnp.transpose(index, (1, 0, 2)).reshape(QC, KTOT)
    key_pos = jnp.arange(KTOT, dtype=jnp.int32)
    query_pos = (KTOT - QC + jnp.arange(QC, dtype=jnp.int32)).astype(jnp.int32)
    valid = key_pos[None, :] <= query_pos[:, None]
    masked = jnp.where(valid, main_target, jnp.float32(0.0))
    mass = jnp.sum(masked, axis=1)
    entropy_sum = jnp.sum(masked * jnp.log(main_target), axis=1)
    cross = jnp.sum(masked * index, axis=1)
    row_max = jnp.max(jnp.where(valid, index, -jnp.inf), axis=1)
    expo = jnp.where(valid, jnp.exp(index - row_max[:, None]), jnp.float32(0.0))
    denom = jnp.sum(expo, axis=1)
    loss_rows = entropy_sum / mass - jnp.log(mass) - cross / mass + row_max + jnp.log(denom)
    grad_index = (expo / denom[:, None] - masked / mass[:, None]) / QC
    grad_blocks = jnp.transpose(grad_index.reshape(QC, N_CTX, KDEV), (1, 0, 2))

    def back_block(carry, inputs):
        block, grad_block = inputs
        keys_f = block.astype(jnp.float32)
        logits = jnp.einsum("tjd,sd->tjs", queries_f, keys_f, precision=highest) * scale_width
        weight_grad = carry[1] + jnp.einsum("ts,tjs->tj", grad_block, jnp.maximum(logits, 0.0), precision=highest) * scale_heads
        logit_grad = (grad_block[:, None, :] * head_weights[:, :, None] * scale_heads * jnp.where(logits > 0, 1.0, 0.0)).astype(jnp.bfloat16)
        logit_grad = lax.optimization_barrier(logit_grad).astype(jnp.float32)
        query_grad = carry[0] + jnp.einsum("tjs,sd->tjd", logit_grad, keys_f, precision=highest) * scale_width
        key_grad = jnp.einsum("tjs,tjd->sd", logit_grad, queries_f, precision=highest) * scale_width
        return (query_grad, weight_grad), key_grad

    start = (jnp.zeros((QC, H, DI), jnp.float32), jnp.zeros((QC, H), jnp.float32))
    (grad_queries, grad_weights), grad_keys = lax.scan(back_block, start, (key_blocks, grad_blocks))
    return grad_queries, grad_weights, grad_keys.reshape(KTOT, DI), loss_rows
```

```python
import functools

import jax
import jax.numpy as jnp
from jax import lax
from jax.experimental import pallas as pl
from jax.experimental.pallas import tpu as pltpu
from jax.sharding import Mesh, PartitionSpec as P

H = 64
T = 64
JL = 32
D = 128
S = 1024
ROWS = T * JL
POS = 131072 - T
SCALE = (D**-0.5) * (H**-0.5)
CTX = ("z", "yl", "x", "c")
CHIPS = ("z", "yl", "x")
N_CHIPS = 64
VMEM = 48 * 1024 * 1024
NT = (((1,), (1,)), ((), ()))


def params():
    return pltpu.CompilerParams(vmem_limit_bytes=VMEM)


def whole(shape):
    return pl.BlockSpec(shape, lambda *_: (0,) * len(shape))


def score_kernel(q_ref, w_ref, k_ref, out_ref):
    width = out_ref.shape[1]
    acc = jnp.zeros((T, width), jnp.float32)
    w = w_ref[...]
    step = 8
    for j0 in range(0, JL, step):
        logits = lax.dot_general(
            q_ref[j0 * T : (j0 + step) * T, :], k_ref[...], NT, preferred_element_type=jnp.float32
        )
        for j in range(step):
            part = jnp.maximum(logits[j * T : (j + 1) * T, :], 0.0)
            acc = acc + w[:, j0 + j : j0 + j + 1] * part
    out_ref[...] = acc * SCALE


def score(q, w, k):
    tile = 256
    return pl.pallas_call(
        score_kernel,
        grid=(S // tile,),
        in_specs=[whole((ROWS, D)), whole((T, JL)), pl.BlockSpec((tile, D), lambda i: (i, 0))],
        out_specs=pl.BlockSpec((T, tile), lambda i: (0, i)),
        out_shape=jax.ShapeDtypeStruct((T, S), jnp.float32),
        compiler_params=params(),
        name="score",
    )(q, w, k)


def valid_mask(ctx):
    key = ctx * S + lax.broadcasted_iota(jnp.int32, (T, S), 1)
    query = POS + lax.broadcasted_iota(jnp.int32, (T, S), 0)
    return key <= query


def stats_kernel(ctx_ref, mine_ref, other_ref, target_ref, index_ref, stats_ref):
    index = mine_ref[...] + other_ref[...]
    index_ref[...] = index
    valid = valid_mask(ctx_ref[0])
    target = target_ref[...]
    masked = jnp.where(valid, target, 0.0)
    row_max = jnp.max(jnp.where(valid, index, -jnp.inf), axis=1, keepdims=True)
    denom = jnp.sum(jnp.where(valid, jnp.exp(index - row_max), 0.0), axis=1, keepdims=True)
    mass = jnp.sum(masked, axis=1, keepdims=True)
    entropy = jnp.sum(masked * jnp.log(target), axis=1, keepdims=True)
    cross = jnp.sum(masked * index, axis=1, keepdims=True)
    lane = lax.broadcasted_iota(jnp.int32, (T, 128), 1)
    packed = jnp.zeros((T, 128), jnp.float32)
    for i, column in enumerate((row_max, denom, mass, entropy, cross)):
        packed = jnp.where(lane == i, column, packed)
    packed = jnp.concatenate([packed, jnp.zeros((128 - T, 128), jnp.float32)], axis=0)
    stats_ref[...] = jnp.transpose(packed)[:8, :]


def local_stats(ctx, mine, other, target):
    return pl.pallas_call(
        stats_kernel,
        in_specs=[pl.BlockSpec(memory_space=pltpu.SMEM)] + [pl.BlockSpec(memory_space=pltpu.VMEM)] * 3,
        out_specs=[pl.BlockSpec(memory_space=pltpu.VMEM)] * 2,
        out_shape=[
            jax.ShapeDtypeStruct((T, S), jnp.float32),
            jax.ShapeDtypeStruct((8, 128), jnp.float32),
        ],
        compiler_params=params(),
        name="stats",
    )(ctx, mine, other, target)


def grad_index_of(ctx, index, target, stats):
    columns = jnp.transpose(jnp.concatenate([stats, jnp.zeros((120, 128), jnp.float32)], axis=0))[:T, :]
    row_max, denom, mass = columns[:, 0:1], columns[:, 1:2], columns[:, 2:3]
    gap = jnp.exp(index - row_max) / denom - target / mass
    return jnp.where(valid_mask(ctx), gap, 0.0) * (SCALE / T)


def query_kernel(who_ref, index_ref, target_ref, stats_ref, q_ref, k_ref, out_ref, g_ref):
    @pl.when(pl.program_id(0) == 0)
    def _():
        g_ref[...] = grad_index_of(who_ref[0], index_ref[...], target_ref[...], stats_ref[...])

    heads = q_ref.shape[0] // T
    logits = lax.dot_general(q_ref[...], k_ref[...], NT, preferred_element_type=jnp.float32)
    g = jnp.concatenate([g_ref[...]] * heads, axis=0)
    picked = jnp.where(logits > 0.0, g, 0.0).astype(jnp.bfloat16)
    out_ref[...] = jnp.dot(picked, k_ref[...], preferred_element_type=jnp.float32)


def query_grads(who, index, target, stats, q, k):
    block = 4 * T
    steps = ROWS // block
    grid_spec = pltpu.PrefetchScalarGridSpec(
        num_scalar_prefetch=1,
        grid=(steps,),
        in_specs=[
            whole((T, S)),
            whole((T, S)),
            whole((8, 128)),
            pl.BlockSpec((block, D), lambda i, who: ((i + who[1] * (steps // 2)) % steps, 0)),
            whole((S, D)),
        ],
        out_specs=pl.BlockSpec((block, D), lambda i, who: (i, 0)),
        scratch_shapes=[pltpu.VMEM((T, S), jnp.float32)],
    )
    return pl.pallas_call(
        query_kernel,
        grid_spec=grid_spec,
        out_shape=jax.ShapeDtypeStruct((ROWS, D), jnp.float32),
        compiler_params=params(),
        name="query_grads",
    )(who, index, target, stats, q, k)


def key_kernel(who_ref, index_ref, target_ref, stats_ref, q_ref, qw_ref, k_ref, out_ref, g_ref):
    @pl.when(pl.program_id(0) == 0)
    def _():
        g = grad_index_of(who_ref[0], index_ref[...], target_ref[...], stats_ref[...])
        g_ref[...] = jnp.transpose(jnp.concatenate([g, g], axis=0))

    tile = k_ref.shape[0]
    g = g_ref[pl.ds(pl.program_id(0) * tile, tile), :]
    acc = jnp.zeros((tile, D), jnp.float32)
    span = 1024
    for r in range(0, ROWS, span):
        logits = lax.dot_general(
            k_ref[...], q_ref[r : r + span, :], NT, preferred_element_type=jnp.float32
        )
        picked = jnp.where(logits > 0.0, jnp.concatenate([g] * (span // 128), axis=1), 0.0)
        acc = acc + jnp.dot(
            picked.astype(jnp.bfloat16), qw_ref[r : r + span, :], preferred_element_type=jnp.float32
        )
    out_ref[...] = acc


def key_grads(who, index, target, stats, q, qw, k):
    tile = 256
    return pl.pallas_call(
        key_kernel,
        grid=(S // tile,),
        in_specs=[
            pl.BlockSpec(memory_space=pltpu.SMEM),
            whole((T, S)),
            whole((T, S)),
            whole((8, 128)),
            whole((ROWS, D)),
            whole((ROWS, D)),
            pl.BlockSpec((tile, D), lambda i: (i, 0)),
        ],
        out_specs=pl.BlockSpec((tile, D), lambda i: (i, 0)),
        out_shape=jax.ShapeDtypeStruct((S, D), jnp.float32),
        scratch_shapes=[pltpu.VMEM((S, 128), jnp.float32)],
        compiler_params=params(),
        name="key_grads",
    )(who, index, target, stats, q, qw, k)


def merge(stats):
    row_max = jnp.max(stats[:, 0], axis=0)
    denom = jnp.sum(stats[:, 1] * jnp.exp(stats[:, 0] - row_max), axis=0)
    rest = jnp.sum(stats[:, 2:], axis=0)
    return jnp.concatenate([row_max[None], denom[None], rest], axis=0)


def on_device(index_queries, head_weights, index_keys, main_target):
    swap = [(0, 1), (1, 0)]
    core = lax.axis_index("c")
    ctx = lax.axis_index(CTX)
    who = jnp.stack([ctx, core]).astype(jnp.int32)
    q = index_queries.transpose(1, 0, 2).reshape(ROWS, D)
    partial_index = score(q, head_weights, index_keys)
    other_index = lax.ppermute(partial_index, "yh", swap)
    index, stats = local_stats(who, partial_index, other_index, main_target)

    pair = jnp.stack([stats, lax.ppermute(stats, "c", swap)])
    pair = merge(pair)
    spread = jnp.broadcast_to(pair[None], (N_CHIPS, 8, 128))
    stats = merge(lax.all_to_all(spread, CHIPS, 0, 0, tiled=True))
    row_max, denom, mass, entropy, cross = (stats[i, :T] for i in range(5))
    loss_rows = entropy / mass - jnp.log(mass) - cross / mass + row_max + jnp.log(denom)

    part = query_grads(who, index, main_target, stats, q, index_keys)
    half = ROWS // 2
    mine = part[:half] + lax.ppermute(part[half:], "c", swap)
    chunks = lax.all_to_all(mine.reshape(N_CHIPS, half // N_CHIPS, D), CHIPS, 0, 0, tiled=True)
    chunk = jnp.sum(chunks, axis=0)

    weighted = (head_weights.T.reshape(ROWS, 1) * q.astype(jnp.float32)).astype(jnp.bfloat16)
    key_part = key_grads(who, index, main_target, stats, q, weighted, index_keys)
    grad_keys = key_part + lax.ppermute(key_part, "yh", swap)

    spread = jnp.broadcast_to(chunk[None], (N_CHIPS,) + chunk.shape)
    mine = lax.all_to_all(spread, CHIPS, 0, 0, tiled=True).reshape(half, D)
    other = lax.ppermute(mine, "c", swap)
    first = jnp.where(core == 0, mine, other)
    second = jnp.where(core == 0, other, mine)
    total = jnp.concatenate([first, second], axis=0).reshape(JL, T, D).transpose(1, 0, 2)
    grad_queries = total * head_weights[:, :, None]
    grad_weights = jnp.sum(total * index_queries.astype(jnp.float32), axis=2)
    return grad_queries, grad_weights, grad_keys, loss_rows


def solution(mesh):
    fine = Mesh(mesh.devices.reshape(8, 2, 4, 2, 2), CTX + ("yh",))
    return jax.shard_map(
        on_device,
        mesh=fine,
        in_specs=(P(None, "yh", None), P(None, "yh"), P(CTX, None), P(None, CTX)),
        out_specs=(P(None, "yh", None), P(None, "yh"), P(CTX, None), P()),
        check_vma=False,
    )
```

```python
import jax
import jax.numpy as jnp
from jax import lax
from jax.experimental import pallas as pl
from jax.experimental.pallas import tpu as pltpu
from jax.sharding import Mesh, PartitionSpec as P

H = 64
T = 64
JL = 32
D = 128
S = 1024
ROWS = T * JL
HALF = ROWS // 2
POS = 131072 - T
SCALE = (D**-0.5) * (H**-0.5)
CTX = ("zh", "zl", "yl", "x", "c")
NEAR = ("zl", "yl", "x")
PLANE = ("zl", "x")
FAR = "zh"
N_NEAR = 16
N_PLANE = 8
N_X = 4
N_FAR = 4
CHUNK = HALF // N_NEAR
KEY_ROWS = S
VMEM = 48 * 1024 * 1024
SCORE_VMEM = 60 * 1024 * 1024
NT = (((1,), (1,)), ((), ()))
IN_VMEM = pl.BlockSpec(memory_space=pltpu.VMEM)
IN_HBM = pl.BlockSpec(memory_space=pltpu.HBM)
IN_SMEM = pl.BlockSpec(memory_space=pltpu.SMEM)


def params(limit=VMEM):
    return pltpu.CompilerParams(vmem_limit_bytes=limit)


def f32(*shape):
    return jax.ShapeDtypeStruct(shape, jnp.float32)


def whole(shape):
    return pl.BlockSpec(shape, lambda *_: (0,) * len(shape))


def cost(flops, nbytes):
    return pl.CostEstimate(flops=flops, bytes_accessed=nbytes, transcendentals=0)


def columns_of(rows):
    width = rows[0].shape[1]
    filled = jnp.concatenate(rows + [jnp.zeros((128 - len(rows), width), jnp.float32)], axis=0)
    if width < 128:
        filled = jnp.concatenate([filled, jnp.zeros((128, 128 - width), jnp.float32)], axis=1)
    turned = jnp.transpose(filled)
    return [turned[:T, i : i + 1] for i in range(len(rows))]


def score_kernel(q_hbm, w_ref, k_hbm, out_ref, by_head_ref, q_ref, k_ref, q_f32, sems):
    heads, tile, step = JL // 2, 512, 4
    k_copy = pltpu.make_async_copy(k_hbm, k_ref, sems.at[2])
    copies = [
        pltpu.make_async_copy(q_hbm.at[:, h * heads : (h + 1) * heads, :], q_ref.at[h], sems.at[h])
        for h in range(2)
    ]
    copies[0].start()
    k_copy.start()
    copies[1].start()
    w = columns_of([w_ref[j : j + 1, :] * SCALE for j in range(JL)])
    for h in range(2):
        copies[h].wait()
        q_f32[...] = q_ref[h].astype(jnp.float32).reshape(HALF, D)
        for j in range(heads):
            at = h * HALF + j * T
            by_head_ref[at : at + T, :] = q_f32[pl.ds(j, T, stride=heads), :].astype(jnp.bfloat16)
        if h == 0:
            k_copy.wait()
        for s in range(0, S, tile):
            acc = jnp.zeros((T, tile), jnp.float32) if h == 0 else out_ref[:, s : s + tile]
            for j0 in range(h * heads, (h + 1) * heads, step):
                logits = lax.dot_general(
                    by_head_ref[j0 * T : (j0 + step) * T, :],
                    k_ref[s : s + tile, :],
                    NT,
                    preferred_element_type=jnp.float32,
                )
                for j in range(step):
                    acc = acc + w[j0 + j] * jnp.maximum(logits[j * T : (j + 1) * T, :], 0.0)
            out_ref[:, s : s + tile] = acc


def score(q, w, k):
    return pl.pallas_call(
        score_kernel,
        in_specs=[IN_HBM, IN_VMEM, IN_HBM],
        out_specs=[IN_VMEM] * 2,
        out_shape=[f32(T, S), jax.ShapeDtypeStruct((ROWS, D), jnp.bfloat16)],
        scratch_shapes=[
            pltpu.VMEM((2, T, JL // 2, D), jnp.bfloat16),
            pltpu.VMEM((S, D), jnp.bfloat16),
            pltpu.VMEM((HALF, D), jnp.float32),
            pltpu.SemaphoreType.DMA((3,)),
        ],
        compiler_params=params(SCORE_VMEM),
        name="score",
    )(q, w, k)


def valid_mask(ctx):
    key = ctx * S + lax.broadcasted_iota(jnp.int32, (T, S), 1)
    query = POS + lax.broadcasted_iota(jnp.int32, (T, S), 0)
    return key <= query


def target_kernel(who_ref, target_ref, index_ref, w_ref, q_ref, normal_ref, sums_ref, held_ref, weighted_ref):
    held_ref[...] = index_ref[...]
    w = columns_of([w_ref[j : j + 1, :] for j in range(JL)])
    for j in range(JL):
        at = slice(j * T, (j + 1) * T)
        weighted_ref[at, :] = (q_ref[at, :].astype(jnp.float32) * w[j]).astype(jnp.bfloat16)
    valid = valid_mask(who_ref[0])
    target = target_ref[...]
    masked = jnp.where(valid, target, 0.0)
    mass = jnp.sum(masked, axis=1, keepdims=True)
    entropy = jnp.sum(masked * jnp.log(target), axis=1, keepdims=True)
    normal_ref[...] = masked * (1.0 / mass)
    lane = lax.broadcasted_iota(jnp.int32, (T, 128), 1)
    sums_ref[...] = jnp.where(lane == 0, mass, entropy)


def target_sums(who, target, partial_index, w, q):
    return pl.pallas_call(
        target_kernel,
        in_specs=[IN_SMEM] + [IN_VMEM] * 4,
        out_specs=[IN_VMEM] * 4,
        out_shape=[f32(T, S), f32(T, 128), f32(T, S), jax.ShapeDtypeStruct((ROWS, D), jnp.bfloat16)],
        compiler_params=params(),
        name="target",
    )(who, target, partial_index, w, q)


def stats_kernel(who_ref, mine_ref, other_ref, target_ref, sums_ref, index_ref, stats_ref, parts_ref):
    index = mine_ref[...] + other_ref[...]
    index_ref[...] = index
    valid = valid_mask(who_ref[0])
    target = target_ref[...]
    row_max = jnp.max(jnp.where(valid, index, -jnp.inf), axis=1, keepdims=True)
    expo = jnp.where(valid, jnp.exp(index - row_max), 0.0)
    denom = jnp.sum(expo, axis=1, keepdims=True)
    mass, entropy = sums_ref[:, 0:1], sums_ref[:, 1:2]
    cross = mass * jnp.sum(target * index, axis=1, keepdims=True)
    lane = lax.broadcasted_iota(jnp.int32, (T, 128), 1)
    packed = jnp.zeros((T, 128), jnp.float32)
    soft = expo * (1.0 / denom)
    peaks = (jnp.sum(x * x, axis=1, keepdims=True) for x in (soft, target))
    mixed = jnp.where(next(peaks) <= 4.0 * next(peaks), 1.0, 0.0)
    for i, column in enumerate((row_max, denom, mass, entropy, cross, mixed)):
        packed = jnp.where(lane == i, column, packed)
    packed = jnp.concatenate([packed, jnp.zeros((128 - T, 128), jnp.float32)], axis=0)
    stats_ref[...] = jnp.transpose(packed)[:8, :]
    parts_ref[0] = soft.astype(jnp.bfloat16)
    parts_ref[1] = (mixed * soft - target).astype(jnp.bfloat16)


def local_stats(who, mine, other, target, sums):
    return pl.pallas_call(
        stats_kernel,
        in_specs=[IN_SMEM] + [IN_VMEM] * 4,
        out_specs=[IN_VMEM] * 3,
        out_shape=[f32(T, S), f32(8, 128), jax.ShapeDtypeStruct((2, T, S), jnp.bfloat16)],
        compiler_params=params(),
        name="stats",
    )(who, mine, other, target, sums)


def query_kernel(who_ref, parts_ref, stats_ref, q_ref, k_ref, out_ref):
    block = 4 * T
    for r in range(0, HALF, block):
        at = pl.multiple_of(who_ref[0] * HALF + r, block)
        logits = lax.dot_general(
            q_ref[pl.ds(at, block), :], k_ref[...], NT, preferred_element_type=jnp.float32
        )
        positive = logits.astype(jnp.bfloat16) > 0.0
        for i in range(2):
            part = jnp.concatenate([parts_ref[i]] * (block // T), axis=0)
            picked = jnp.where(positive, part, jnp.zeros_like(part))
            at = slice(i * HALF + r, i * HALF + r + block)
            out_ref[at, :] = jnp.dot(picked, k_ref[...], preferred_element_type=jnp.float32)
    out_ref[ROWS:, :] = stats_ref[...]


def query_sums(half, parts, stats, q, k, name):
    return pl.pallas_call(
        query_kernel,
        in_specs=[IN_SMEM] + [IN_VMEM] * 4,
        out_specs=IN_VMEM,
        out_shape=f32(ROWS + 8, D),
        compiler_params=params(),
        cost_estimate=cost(6 * HALF * S * D, 4 << 20),
        name=name,
    )(half, parts, stats, q, k)


def merge(stats):
    row_max = stats[0][0:1]
    for s in stats[1:]:
        row_max = jnp.maximum(row_max, s[0:1])
    denom, rest = 0.0, 0.0
    for s in stats:
        denom = denom + s[1:2] * jnp.exp(s[0:1] - row_max)
        rest = rest + s[2:8]
    return jnp.concatenate([row_max, denom, rest], axis=0)


def shares(part, total):
    return part[1:2] * jnp.exp(part[0:1] - total[0:1]) / total[1:2], part[2:3] / total[2:3]


def pack_kernel(keep_ref, recv_ref, out_ref):
    mine, other = keep_ref[ROWS:, :], recv_ref[ROWS:, :]
    chip = merge([mine, other])
    rows = [*shares(mine, chip), mine[5:6], *shares(other, chip), other[5:6]]
    soft_a, target_a, mixed_a, soft_b, target_b, mixed_b = columns_of(rows)
    gap_a, gap_b = soft_a - mixed_a * target_a, soft_b - mixed_b * target_b
    for i in range(N_NEAR):
        at, too = slice(i * CHUNK, (i + 1) * CHUNK), slice(HALF + i * CHUNK, HALF + (i + 1) * CHUNK)
        a, b = keep_ref[at, :], recv_ref[at, :]
        out_ref[i, :CHUNK, :] = soft_a * a + soft_b * b
        gap = gap_a * a + gap_b * b + target_a * keep_ref[too, :] + target_b * recv_ref[too, :]
        out_ref[i, CHUNK : 2 * CHUNK, :] = gap
        out_ref[i, 2 * CHUNK :, :] = chip


def pack(keep, recv):
    return pl.pallas_call(
        pack_kernel,
        in_specs=[IN_VMEM] * 2,
        out_specs=IN_VMEM,
        out_shape=f32(N_NEAR, 2 * CHUNK + 8, 128),
        compiler_params=params(),
        name="pack",
    )(keep, recv)


def combine_parts(refs):
    parts = [ref[2 * CHUNK :, :] for ref in refs]
    total = merge(parts)
    columns = columns_of([row for part in parts for row in shares(part, total)])
    soft_sum, gap_sum = 0.0, 0.0
    for i, ref in enumerate(refs):
        soft, target = columns[2 * i], columns[2 * i + 1]
        a = ref[:CHUNK, :]
        soft_sum = soft_sum + soft * a
        gap_sum = gap_sum + (soft - target) * a + target * ref[CHUNK : 2 * CHUNK, :]
    return total, soft_sum, gap_sum


def near_kernel(in_ref, out_ref):
    total, soft_sum, gap_sum = combine_parts([in_ref.at[i] for i in range(N_NEAR)])
    out_ref[:CHUNK, :] = soft_sum
    out_ref[CHUNK : 2 * CHUNK, :] = gap_sum
    out_ref[2 * CHUNK :, :] = total


def combine_near(received):
    return pl.pallas_call(
        near_kernel,
        in_specs=[IN_VMEM],
        out_specs=IN_VMEM,
        out_shape=f32(2 * CHUNK + 8, D),
        compiler_params=params(),
        name="combine_near",
    )(received)


def far_kernel(who_ref, a_ref, b_ref, c_ref, d_ref, w_ref, q_ref, out_ref, stats_ref, loss_ref):
    total, _, gap_sum = combine_parts([a_ref, b_ref, c_ref, d_ref])
    row_max, denom, mass, entropy, cross = (total[i : i + 1] for i in range(5))
    stats_ref[...] = total
    loss = entropy / mass - jnp.log(mass) - cross / mass + row_max + jnp.log(denom)
    loss_ref[...] = jnp.broadcast_to(loss, loss_ref.shape)
    gap_sum = gap_sum * (SCALE / T)
    head = who_ref[2]
    scaled = gap_sum * columns_of([w_ref[pl.ds(head, 1), :]])[0]
    q = q_ref[pl.ds(pl.multiple_of(head * T, T), T), :].astype(jnp.float32)
    grads = jnp.broadcast_to(jnp.sum(gap_sum * q, axis=1, keepdims=True), (T, 128))
    grads = jnp.transpose(jnp.concatenate([grads, grads], axis=0))[:8]
    out_ref[:CHUNK, :] = scaled
    out_ref[CHUNK:, :] = grads


def combine_far(who, own, far, w, q):
    return pl.pallas_call(
        far_kernel,
        in_specs=[IN_SMEM] + [IN_VMEM] * 6,
        out_specs=[IN_VMEM] * 3,
        out_shape=[f32(CHUNK + 8, D), f32(8, 128), f32(8, 128)],
        compiler_params=params(),
        name="combine_far",
    )(who, own, *far, w, q)


def spread_kernel(who_ref, mine_ref, other_ref, out_ref):
    size = CHUNK + 8
    first = who_ref[3] == 0
    for p in range(N_PLANE):
        out_ref[p, :size, :] = jnp.where(first, mine_ref[...], other_ref[...])
        out_ref[p, size:, :] = jnp.where(first, other_ref[...], mine_ref[...])


def spread(who, mine, other):
    return pl.pallas_call(
        spread_kernel,
        in_specs=[IN_SMEM] + [IN_VMEM] * 2,
        out_specs=IN_VMEM,
        out_shape=f32(N_PLANE, 2 * (CHUNK + 8), D),
        compiler_params=params(),
        name="spread",
    )(who, mine, other)


def chunks_of():
    for p in range(N_PLANE):
        for y in range(2):
            yield (p // N_X * 2 + y) * N_X + p % N_X, p, y * (CHUNK + 8)


def place_half(half, at, out_hbm, rows_ref, sem):
    for j, p, r in chunks_of():
        ref, i = at(p)
        rows_ref[pl.ds(j, T, stride=N_NEAR), :] = ref[i, r : r + CHUNK, :]
    to = out_hbm.at[:, pl.ds(pl.multiple_of(half * N_NEAR, N_NEAR), N_NEAR), :]
    copy = pltpu.make_async_copy(rows_ref.reshape(T, N_NEAR, D), to, sem)
    copy.start()
    return copy


def first_kernel(who_ref, mine_ref, out_hbm, rows_ref, sem):
    place_half(who_ref[1], lambda p: (mine_ref, p), out_hbm, rows_ref, sem).wait()


def last_kernel(who_ref, mine_ref, lower_ref, upper_ref, begun_hbm, out_hbm, weights_ref, rows_ref, sem):
    def mine_at(p):
        return mine_ref, p

    def other_at(p):
        return (lower_ref, p) if p < N_PLANE // 2 else (upper_ref, p - N_PLANE // 2)

    copy = place_half(1 - who_ref[1], other_at, out_hbm, rows_ref, sem)

    def emit(first, second):
        for half, at in enumerate((first, second)):
            for j, p, r in chunks_of():
                ref, i = at(p)
                row = half * N_NEAR + j
                weights_ref[row : row + 1, :] = ref[i, r + CHUNK : r + CHUNK + 1, :T]

    pl.when(who_ref[1] == 0)(lambda: emit(mine_at, other_at))
    pl.when(who_ref[1] == 1)(lambda: emit(other_at, mine_at))
    copy.wait()


HALF_SCRATCH = [pltpu.VMEM((HALF, D), jnp.float32), pltpu.SemaphoreType.DMA(())]


def place_mine(who, mine):
    return pl.pallas_call(
        first_kernel,
        in_specs=[IN_SMEM, IN_VMEM],
        out_specs=IN_HBM,
        out_shape=f32(T, JL, D),
        scratch_shapes=HALF_SCRATCH,
        compiler_params=params(),
        name="place_mine",
    )(who, mine)


def place_other(who, mine, other, begun):
    return pl.pallas_call(
        last_kernel,
        in_specs=[IN_SMEM, IN_VMEM, IN_VMEM, IN_VMEM, IN_HBM],
        out_specs=[IN_HBM, IN_VMEM],
        out_shape=[f32(T, JL, D), f32(JL, T)],
        scratch_shapes=HALF_SCRATCH,
        input_output_aliases={4: 0},
        compiler_params=params(),
        name="place_other",
    )(who, mine, *other, begun)


def key_kernel(who_ref, index_ref, target_ref, stats_ref, q_ref, weighted_ref, k_ref, out_ref):
    row_max, denom, mass = columns_of([stats_ref[i : i + 1, :] for i in range(3)])
    gap = jnp.exp(index_ref[...] - row_max) * (1.0 / denom) - target_ref[...] * (1.0 / mass)
    gap = jnp.where(valid_mask(who_ref[0]), gap, 0.0) * (SCALE / T)
    tile, span = 256, 1024
    for s in range(0, S, tile):
        g = gap[:, s : s + tile]
        g = jnp.transpose(jnp.concatenate([g, g], axis=0))
        acc = jnp.zeros((tile, D), jnp.float32)
        for r in range(0, ROWS, span):
            logits = lax.dot_general(
                k_ref[s : s + tile, :], q_ref[r : r + span, :], NT, preferred_element_type=jnp.float32
            )
            picked = jnp.where(logits > 0.0, jnp.concatenate([g] * (span // 128), axis=1), 0.0)
            acc = acc + jnp.dot(
                picked.astype(jnp.bfloat16), weighted_ref[r : r + span, :], preferred_element_type=jnp.float32
            )
        out_ref[s : s + tile, :] = acc


def key_grads(who, index, target, stats, q, weighted, k):
    return pl.pallas_call(
        key_kernel,
        in_specs=[IN_SMEM] + [IN_VMEM] * 6,
        out_specs=IN_VMEM,
        out_shape=f32(KEY_ROWS, D),
        compiler_params=params(),
        cost_estimate=cost(4 * ROWS * S * D, 4 << 20),
        name="key_grads",
    )(who, index, target, stats, q, weighted, k)


def on_device(index_queries, head_weights, index_keys, main_target):
    swap = [(0, 1), (1, 0)]
    core = lax.axis_index("c")
    head = core * N_NEAR + lax.axis_index(NEAR)
    who = jnp.stack([lax.axis_index(CTX), core, head, lax.axis_index("yl")]).astype(jnp.int32)
    w = head_weights.T
    partial_index, q = score(index_queries, w, index_keys)
    other_index = lax.ppermute(partial_index, "yh", swap)
    target, target_sum, held_index, weighted = target_sums(who, main_target, partial_index, w, q)
    index, stats, parts = local_stats(who, held_index, other_index, target, target_sum)

    send = query_sums(1 - who[1:2], parts, stats, q, index_keys, "query_sums_send")
    recv = lax.ppermute(send, "c", swap)
    keep = query_sums(who[1:2], parts, stats, q, index_keys, "query_sums_keep")
    near = lax.all_to_all(pack(keep, recv), NEAR, 0, 0, tiled=True)
    own = combine_near(near)
    far = [lax.ppermute(own, FAR, [(i, i ^ d) for i in range(N_FAR)]) for d in range(1, N_FAR)]
    chunk, total_stats, loss = combine_far(who, own, far, w, q)

    other_chunk = lax.ppermute(chunk, "yl", swap)
    key_part = key_grads(who, index, main_target, total_stats, q, weighted, index_keys)
    other_key_part = lax.ppermute(key_part, "yh", swap)
    other_chunk, _ = lax.optimization_barrier((other_chunk, key_part))
    mine = lax.all_to_all(spread(who, chunk, other_chunk), PLANE, 0, 0, tiled=True)
    half = N_PLANE // 2
    other = [lax.ppermute(x, "c", swap) for x in (mine[:half], mine[half:])]
    grad_queries, grad_weights = place_other(who, mine, other, place_mine(who, mine))
    grad_weights, key_part = lax.optimization_barrier((grad_weights, key_part))
    return grad_queries, grad_weights.T, key_part[:S] + other_key_part[:S], loss[0, :T]


def solution(mesh):
    fine = Mesh(mesh.devices.reshape(N_FAR, 2, 2, 4, 2, 2), CTX + ("yh",))
    return jax.shard_map(
        on_device,
        mesh=fine,
        in_specs=(P(None, "yh", None), P(None, "yh"), P(CTX, None), P(None, CTX)),
        out_specs=(P(None, "yh", None), P(None, "yh"), P(CTX, None), P()),
        check_vma=False,
    )
```

```python
import jax
import jax.numpy as jnp
from jax import lax
from jax.experimental import pallas as pl
from jax.experimental.pallas import tpu as pltpu
from jax.sharding import Mesh, PartitionSpec as P

H = 64
T = 64
JL = 32
D = 128
S = 1024
ROWS = T * JL
HALF = ROWS // 2
POS = 131072 - T
SCALE = (D**-0.5) * (H**-0.5)
CTX = ("zh", "zl", "yl", "x", "c")
NEAR = ("zl", "yl", "x")
FAR = "zh"
N_NEAR = 16
N_FAR = 4
CHUNK = HALF // N_NEAR
KEY_ROWS = S
VMEM = 48 * 1024 * 1024
SCORE_VMEM = 60 * 1024 * 1024
NT = (((1,), (1,)), ((), ()))
IN_VMEM = pl.BlockSpec(memory_space=pltpu.VMEM)
IN_HBM = pl.BlockSpec(memory_space=pltpu.HBM)
IN_SMEM = pl.BlockSpec(memory_space=pltpu.SMEM)


def params(limit=VMEM):
    return pltpu.CompilerParams(vmem_limit_bytes=limit)


def f32(*shape):
    return jax.ShapeDtypeStruct(shape, jnp.float32)


def whole(shape):
    return pl.BlockSpec(shape, lambda *_: (0,) * len(shape))


def cost(flops, nbytes):
    return pl.CostEstimate(flops=flops, bytes_accessed=nbytes, transcendentals=0)


def columns_of(rows):
    width = rows[0].shape[1]
    filled = jnp.concatenate(rows + [jnp.zeros((128 - len(rows), width), jnp.float32)], axis=0)
    if width < 128:
        filled = jnp.concatenate([filled, jnp.zeros((128, 128 - width), jnp.float32)], axis=1)
    turned = jnp.transpose(filled)
    return [turned[:T, i : i + 1] for i in range(len(rows))]


def score_kernel(q_hbm, w_ref, k_hbm, out_ref, by_head_ref, q_ref, k_ref, q_f32, sems):
    heads, tile, step = JL // 2, 512, 4
    k_copy = pltpu.make_async_copy(k_hbm, k_ref, sems.at[2])
    copies = [
        pltpu.make_async_copy(q_hbm.at[:, h * heads : (h + 1) * heads, :], q_ref.at[h], sems.at[h])
        for h in range(2)
    ]
    copies[0].start()
    k_copy.start()
    copies[1].start()
    w = columns_of([w_ref[j : j + 1, :] * SCALE for j in range(JL)])
    for h in range(2):
        copies[h].wait()
        q_f32[...] = q_ref[h].astype(jnp.float32).reshape(HALF, D)
        for j in range(heads):
            at = h * HALF + j * T
            by_head_ref[at : at + T, :] = q_f32[pl.ds(j, T, stride=heads), :].astype(jnp.bfloat16)
        if h == 0:
            k_copy.wait()
        for s in range(0, S, tile):
            acc = jnp.zeros((T, tile), jnp.float32) if h == 0 else out_ref[:, s : s + tile]
            for j0 in range(h * heads, (h + 1) * heads, step):
                logits = lax.dot_general(
                    by_head_ref[j0 * T : (j0 + step) * T, :],
                    k_ref[s : s + tile, :],
                    NT,
                    preferred_element_type=jnp.float32,
                )
                for j in range(step):
                    acc = acc + w[j0 + j] * jnp.maximum(logits[j * T : (j + 1) * T, :], 0.0)
            out_ref[:, s : s + tile] = acc


def score(q, w, k):
    return pl.pallas_call(
        score_kernel,
        in_specs=[IN_HBM, IN_VMEM, IN_HBM],
        out_specs=[IN_VMEM] * 2,
        out_shape=[f32(T, S), jax.ShapeDtypeStruct((ROWS, D), jnp.bfloat16)],
        scratch_shapes=[
            pltpu.VMEM((2, T, JL // 2, D), jnp.bfloat16),
            pltpu.VMEM((S, D), jnp.bfloat16),
            pltpu.VMEM((HALF, D), jnp.float32),
            pltpu.SemaphoreType.DMA((3,)),
        ],
        compiler_params=params(SCORE_VMEM),
        name="score",
    )(q, w, k)


def valid_mask(ctx):
    key = ctx * S + lax.broadcasted_iota(jnp.int32, (T, S), 1)
    query = POS + lax.broadcasted_iota(jnp.int32, (T, S), 0)
    return key <= query


def target_kernel(who_ref, target_ref, index_ref, w_ref, q_ref, normal_ref, sums_ref, held_ref, weighted_ref, payload_ref):
    held_ref[...] = index_ref[...]
    w = columns_of([w_ref[j : j + 1, :] for j in range(JL)])
    for j in range(JL):
        at = slice(j * T, (j + 1) * T)
        weighted_ref[at, :] = (q_ref[at, :].astype(jnp.float32) * w[j]).astype(jnp.bfloat16)
    core = who_ref[1]
    payload_ref[:HALF, :] = q_ref[pl.ds(pl.multiple_of(core * HALF, HALF), HALF), :].astype(jnp.float32)
    part = w_ref[pl.ds(pl.multiple_of(core * N_NEAR, N_NEAR), N_NEAR), :]
    payload_ref[HALF:, :] = jnp.concatenate([part, jnp.zeros((N_NEAR, 128 - T), jnp.float32)], axis=1)
    valid = valid_mask(who_ref[0])
    target = target_ref[...]
    masked = jnp.where(valid, target, 0.0)
    mass = jnp.sum(masked, axis=1, keepdims=True)
    entropy = jnp.sum(masked * jnp.log(target), axis=1, keepdims=True)
    normal_ref[...] = masked * (1.0 / mass)
    lane = lax.broadcasted_iota(jnp.int32, (T, 128), 1)
    sums_ref[...] = jnp.where(lane == 0, mass, entropy)


def target_sums(who, target, partial_index, w, q):
    return pl.pallas_call(
        target_kernel,
        in_specs=[IN_SMEM] + [IN_VMEM] * 4,
        out_specs=[IN_VMEM] * 5,
        out_shape=[
            f32(T, S),
            f32(T, 128),
            f32(T, S),
            jax.ShapeDtypeStruct((ROWS, D), jnp.bfloat16),
            f32(HALF + N_NEAR, D),
        ],
        compiler_params=params(),
        name="target",
    )(who, target, partial_index, w, q)


def stats_kernel(who_ref, mine_ref, other_ref, target_ref, sums_ref, index_ref, stats_ref, parts_ref):
    index = mine_ref[...] + other_ref[...]
    index_ref[...] = index
    valid = valid_mask(who_ref[0])
    target = target_ref[...]
    row_max = jnp.max(jnp.where(valid, index, -jnp.inf), axis=1, keepdims=True)
    expo = jnp.where(valid, jnp.exp(index - row_max), 0.0)
    denom = jnp.sum(expo, axis=1, keepdims=True)
    mass, entropy = sums_ref[:, 0:1], sums_ref[:, 1:2]
    cross = mass * jnp.sum(target * index, axis=1, keepdims=True)
    lane = lax.broadcasted_iota(jnp.int32, (T, 128), 1)
    packed = jnp.zeros((T, 128), jnp.float32)
    soft = expo * (1.0 / denom)
    peaks = (jnp.sum(x * x, axis=1, keepdims=True) for x in (soft, target))
    mixed = jnp.where(next(peaks) <= 4.0 * next(peaks), 1.0, 0.0)
    for i, column in enumerate((row_max, denom, mass, entropy, cross, mixed)):
        packed = jnp.where(lane == i, column, packed)
    packed = jnp.concatenate([packed, jnp.zeros((128 - T, 128), jnp.float32)], axis=0)
    stats_ref[...] = jnp.transpose(packed)[:8, :]
    parts_ref[0] = soft.astype(jnp.bfloat16)
    parts_ref[1] = (mixed * soft - target).astype(jnp.bfloat16)


def local_stats(who, mine, other, target, sums):
    return pl.pallas_call(
        stats_kernel,
        in_specs=[IN_SMEM] + [IN_VMEM] * 4,
        out_specs=[IN_VMEM] * 3,
        out_shape=[f32(T, S), f32(8, 128), jax.ShapeDtypeStruct((2, T, S), jnp.bfloat16)],
        compiler_params=params(),
        name="stats",
    )(who, mine, other, target, sums)


def query_kernel(who_ref, parts_ref, stats_ref, q_ref, k_ref, out_ref):
    block = 4 * T
    for r in range(0, HALF, block):
        at = pl.multiple_of(who_ref[0] * HALF + r, block)
        logits = lax.dot_general(
            q_ref[pl.ds(at, block), :], k_ref[...], NT, preferred_element_type=jnp.float32
        )
        positive = logits.astype(jnp.bfloat16) > 0.0
        for i in range(2):
            part = jnp.concatenate([parts_ref[i]] * (block // T), axis=0)
            picked = jnp.where(positive, part, jnp.zeros_like(part))
            at = slice(i * HALF + r, i * HALF + r + block)
            out_ref[at, :] = jnp.dot(picked, k_ref[...], preferred_element_type=jnp.float32)
    out_ref[ROWS:, :] = stats_ref[...]


def query_sums(half, parts, stats, q, k, name):
    return pl.pallas_call(
        query_kernel,
        in_specs=[IN_SMEM] + [IN_VMEM] * 4,
        out_specs=IN_VMEM,
        out_shape=f32(ROWS + 8, D),
        compiler_params=params(),
        cost_estimate=cost(6 * HALF * S * D, 4 << 20),
        name=name,
    )(half, parts, stats, q, k)


def merge(stats):
    row_max = stats[0][0:1]
    for s in stats[1:]:
        row_max = jnp.maximum(row_max, s[0:1])
    denom, rest = 0.0, 0.0
    for s in stats:
        denom = denom + s[1:2] * jnp.exp(s[0:1] - row_max)
        rest = rest + s[2:8]
    return jnp.concatenate([row_max, denom, rest], axis=0)


def shares(part, total):
    return part[1:2] * jnp.exp(part[0:1] - total[0:1]) / total[1:2], part[2:3] / total[2:3]


def pack_kernel(keep_ref, recv_ref, out_ref):
    mine, other = keep_ref[ROWS:, :], recv_ref[ROWS:, :]
    chip = merge([mine, other])
    rows = [*shares(mine, chip), mine[5:6], *shares(other, chip), other[5:6]]
    soft_a, target_a, mixed_a, soft_b, target_b, mixed_b = columns_of(rows)
    gap_a, gap_b = soft_a - mixed_a * target_a, soft_b - mixed_b * target_b
    for i in range(N_NEAR):
        at, too = slice(i * CHUNK, (i + 1) * CHUNK), slice(HALF + i * CHUNK, HALF + (i + 1) * CHUNK)
        a, b = keep_ref[at, :], recv_ref[at, :]
        out_ref[i, :CHUNK, :] = soft_a * a + soft_b * b
        gap = gap_a * a + gap_b * b + target_a * keep_ref[too, :] + target_b * recv_ref[too, :]
        out_ref[i, CHUNK : 2 * CHUNK, :] = gap
        out_ref[i, 2 * CHUNK :, :] = chip


def pack(keep, recv):
    return pl.pallas_call(
        pack_kernel,
        in_specs=[IN_VMEM] * 2,
        out_specs=IN_VMEM,
        out_shape=f32(N_NEAR, 2 * CHUNK + 8, 128),
        compiler_params=params(),
        name="pack",
    )(keep, recv)


def combine_parts(refs):
    parts = [ref[2 * CHUNK :, :] for ref in refs]
    total = merge(parts)
    columns = columns_of([row for part in parts for row in shares(part, total)])
    soft_sum, gap_sum = 0.0, 0.0
    for i, ref in enumerate(refs):
        soft, target = columns[2 * i], columns[2 * i + 1]
        a = ref[:CHUNK, :]
        soft_sum = soft_sum + soft * a
        gap_sum = gap_sum + (soft - target) * a + target * ref[CHUNK : 2 * CHUNK, :]
    return total, soft_sum, gap_sum


def near_kernel(in_ref, out_ref):
    total, soft_sum, gap_sum = combine_parts([in_ref.at[i] for i in range(N_NEAR)])
    out_ref[:CHUNK, :] = soft_sum
    out_ref[CHUNK : 2 * CHUNK, :] = gap_sum
    out_ref[2 * CHUNK :, :] = total


def combine_near(received):
    return pl.pallas_call(
        near_kernel,
        in_specs=[IN_VMEM],
        out_specs=IN_VMEM,
        out_shape=f32(2 * CHUNK + 8, D),
        compiler_params=params(),
        name="combine_near",
    )(received)


def far_kernel(who_ref, a_ref, b_ref, c_ref, d_ref, w_ref, q_ref, out_ref, stats_ref, loss_ref):
    total, _, gap_sum = combine_parts([a_ref, b_ref, c_ref, d_ref])
    row_max, denom, mass, entropy, cross = (total[i : i + 1] for i in range(5))
    stats_ref[...] = total
    loss = entropy / mass - jnp.log(mass) - cross / mass + row_max + jnp.log(denom)
    loss_ref[...] = jnp.broadcast_to(loss, loss_ref.shape)
    gap_sum = gap_sum * (SCALE / T)
    head = who_ref[2]
    scaled = gap_sum * columns_of([w_ref[pl.ds(head, 1), :]])[0]
    q = q_ref[pl.ds(pl.multiple_of(head * T, T), T), :].astype(jnp.float32)
    grads = jnp.broadcast_to(jnp.sum(gap_sum * q, axis=1, keepdims=True), (T, 128))
    grads = jnp.transpose(jnp.concatenate([grads, grads], axis=0))[:8]
    for p in range(N_NEAR):
        out_ref[p, :CHUNK, :] = scaled
        out_ref[p, CHUNK:, :] = grads


def combine_far(who, own, far, w, q):
    return pl.pallas_call(
        far_kernel,
        in_specs=[IN_SMEM] + [IN_VMEM] * 6,
        out_specs=[IN_VMEM] * 3,
        out_shape=[f32(N_NEAR, CHUNK + 8, D), f32(8, 128), f32(8, 128)],
        compiler_params=params(),
        name="combine_far",
    )(who, own, *far, w, q)


def place_half(half, at, out_hbm, sem):
    copies = []
    for p in range(N_NEAR):
        ref, i = at(p)
        to = out_hbm.at[:, half * N_NEAR + p, :]
        copies.append(pltpu.make_async_copy(ref.at[i, :CHUNK, :], to, sem.at[p]))
    for copy in copies:
        copy.start()
    return copies


def first_kernel(who_ref, mine_ref, out_hbm, sem):
    for copy in place_half(who_ref[1], lambda p: (mine_ref, p), out_hbm, sem):
        copy.wait()


def last_kernel(who_ref, mine_ref, lower_ref, upper_ref, begun_hbm, out_hbm, weights_ref, sem):
    def mine_at(p):
        return mine_ref, p

    def other_at(p):
        return (lower_ref, p) if p < N_NEAR // 2 else (upper_ref, p - N_NEAR // 2)

    copies = place_half(1 - who_ref[1], other_at, out_hbm, sem)

    def emit(first, second):
        for half, at in enumerate((first, second)):
            for p in range(N_NEAR):
                ref, i = at(p)
                row = half * N_NEAR + p
                weights_ref[row : row + 1, :] = ref[i, CHUNK : CHUNK + 1, :T]

    pl.when(who_ref[1] == 0)(lambda: emit(mine_at, other_at))
    pl.when(who_ref[1] == 1)(lambda: emit(other_at, mine_at))
    for copy in copies:
        copy.wait()


HALF_SCRATCH = [pltpu.SemaphoreType.DMA((N_NEAR,))]


def place_mine(who, mine):
    return pl.pallas_call(
        first_kernel,
        in_specs=[IN_SMEM, IN_VMEM],
        out_specs=IN_HBM,
        out_shape=f32(T, JL, D),
        scratch_shapes=HALF_SCRATCH,
        compiler_params=params(),
        name="place_mine",
    )(who, mine)


def place_other(who, mine, other, begun):
    return pl.pallas_call(
        last_kernel,
        in_specs=[IN_SMEM, IN_VMEM, IN_VMEM, IN_VMEM, IN_HBM],
        out_specs=[IN_HBM, IN_VMEM],
        out_shape=[f32(T, JL, D), f32(JL, T)],
        scratch_shapes=HALF_SCRATCH,
        input_output_aliases={4: 0},
        compiler_params=params(),
        name="place_other",
    )(who, mine, *other, begun)


def unpack_kernel(payload_ref, q_ref, weighted_ref):
    w = columns_of([payload_ref[HALF + j : HALF + j + 1, :] for j in range(N_NEAR)])
    for j in range(N_NEAR):
        at = slice(j * T, (j + 1) * T)
        q = payload_ref[at, :]
        q_ref[at, :] = q.astype(jnp.bfloat16)
        weighted_ref[at, :] = (q * w[j]).astype(jnp.bfloat16)


KEY_TILE = 256


def key_sums(gap, k, q_ref, weighted_ref):
    span = 1024
    gap = jnp.concatenate([gap] * (span // 128), axis=1)
    acc = jnp.zeros((KEY_TILE, D), jnp.float32)
    for r in range(0, q_ref.shape[0], span):
        logits = lax.dot_general(k, q_ref[r : r + span, :], NT, preferred_element_type=jnp.float32)
        picked = jnp.where(logits > 0.0, gap, 0.0).astype(jnp.bfloat16)
        acc = acc + jnp.dot(picked, weighted_ref[r : r + span, :], preferred_element_type=jnp.float32)
    return acc


def own_kernel(who_ref, index_ref, target_ref, stats_ref, q_ref, weighted_ref, k_ref, out_ref, gap_ref):
    row_max, denom, mass = columns_of([stats_ref[i : i + 1, :] for i in range(3)])
    gap = jnp.exp(index_ref[...] - row_max) * (1.0 / denom) - target_ref[...] * (1.0 / mass)
    gap = jnp.where(valid_mask(who_ref[0]), gap, 0.0) * (SCALE / T)
    for s in range(0, S, KEY_TILE):
        at = slice(s, s + KEY_TILE)
        turned = jnp.transpose(jnp.concatenate([gap[:, at]] * 2, axis=0))
        gap_ref[at, :] = turned
        out_ref[at, :] = key_sums(turned, k_ref[at, :], q_ref, weighted_ref)


def own_key_grads(who, index, target, stats, q, weighted, k):
    return pl.pallas_call(
        own_kernel,
        in_specs=[IN_SMEM] + [IN_VMEM] * 6,
        out_specs=[IN_VMEM] * 2,
        out_shape=[f32(S, D)] * 2,
        compiler_params=params(),
        cost_estimate=cost(4 * ROWS * S * D, 4 << 20),
        name="own_key_grads",
    )(who, index, target, stats, q, weighted, k)


def other_kernel(
    own_ref, gap_ref, k_ref, payload_a_ref, payload_b_ref, out_hbm,
    q_a_ref, weighted_a_ref, q_b_ref, weighted_b_ref, out_ref, sems,
):
    unpack_kernel(payload_a_ref, q_a_ref, weighted_a_ref)
    unpack_kernel(payload_b_ref, q_b_ref, weighted_b_ref)
    copies = []
    for s in range(0, S, KEY_TILE):
        at = slice(s, s + KEY_TILE)
        gap, k = gap_ref[at, :], k_ref[at, :]
        both = key_sums(gap, k, q_a_ref, weighted_a_ref) + key_sums(gap, k, q_b_ref, weighted_b_ref)
        out_ref[at, :] = own_ref[at, :] + both
        copies.append(pltpu.make_async_copy(out_ref.at[at], out_hbm.at[at], sems.at[s // KEY_TILE]))
        copies[-1].start()
    for copy in copies:
        copy.wait()


def key_grads(own, gap, k, *heads):
    return pl.pallas_call(
        other_kernel,
        in_specs=[IN_VMEM] * 5,
        out_specs=IN_HBM,
        out_shape=f32(S, D),
        scratch_shapes=[pltpu.VMEM((HALF, D), jnp.bfloat16)] * 4
        + [pltpu.VMEM((S, D), jnp.float32), pltpu.SemaphoreType.DMA((S // KEY_TILE,))],
        compiler_params=params(),
        cost_estimate=cost(4 * ROWS * S * D, 4 << 20),
        name="key_grads",
    )(own, gap, k, *heads)


def on_device(index_queries, head_weights, index_keys, main_target):
    swap = [(0, 1), (1, 0)]
    core = lax.axis_index("c")
    head = core * N_NEAR + lax.axis_index(NEAR)
    who = jnp.stack([lax.axis_index(CTX), core, head]).astype(jnp.int32)
    w = head_weights.T
    partial_index, q = score(index_queries, w, index_keys)
    other_index = lax.ppermute(partial_index, "yh", swap)
    target, target_sum, held_index, weighted, payload = target_sums(who, main_target, partial_index, w, q)
    payload = lax.ppermute(payload, "yh", swap)
    payloads = [payload, lax.ppermute(payload, "c", swap)]
    index, stats, parts = local_stats(who, held_index, other_index, target, target_sum)

    send = query_sums(1 - who[1:2], parts, stats, q, index_keys, "query_sums_send")
    recv = lax.ppermute(send, "c", swap)
    keep = query_sums(who[1:2], parts, stats, q, index_keys, "query_sums_keep")
    near = lax.all_to_all(pack(keep, recv), NEAR, 0, 0, tiled=True)
    own = combine_near(near)
    far = [lax.ppermute(own, FAR, [(i, i ^ d) for i in range(N_FAR)]) for d in range(1, N_FAR)]
    chunk, total_stats, loss = combine_far(who, own, far, w, q)

    mine = lax.all_to_all(chunk, NEAR, 0, 0, tiled=True)
    own, gap = own_key_grads(who, index, main_target, total_stats, q, weighted, index_keys)
    grad_keys = key_grads(own, gap, index_keys, *payloads)
    mine, grad_keys = lax.optimization_barrier((mine, grad_keys))
    half = N_NEAR // 2
    other = [lax.ppermute(x, "c", swap) for x in (mine[:half], mine[half:])]
    grad_queries, grad_weights = place_other(who, mine, other, place_mine(who, mine))
    return grad_queries, grad_weights.T, grad_keys, loss[0, :T]


def solution(mesh):
    fine = Mesh(mesh.devices.reshape(N_FAR, 2, 2, 4, 2, 2), CTX + ("yh",))
    return jax.shard_map(
        on_device,
        mesh=fine,
        in_specs=(P(None, "yh", None), P(None, "yh"), P(CTX, None), P(None, CTX)),
        out_specs=(P(None, "yh", None), P(None, "yh"), P(CTX, None), P()),
        check_vma=False,
    )
```

```python
import jax
import jax.numpy as jnp
from jax import lax
from jax.experimental import pallas as pl
from jax.experimental.pallas import tpu as pltpu
from jax.sharding import Mesh, PartitionSpec as P

H = 64
T = 64
JL = 32
D = 128
S = 1024
ROWS = T * JL
HALF = ROWS // 2
POS = 131072 - T
SCALE = (D**-0.5) * (H**-0.5)
CTX = ("zh", "zl", "yl", "x", "c")
NEAR = ("zl", "yl", "x")
FAR = "zh"
N_NEAR = 16
N_FAR = 4
CHUNK = HALF // N_NEAR
KEY_ROWS = S
VMEM = 48 * 1024 * 1024
SCORE_VMEM = 60 * 1024 * 1024
NT = (((1,), (1,)), ((), ()))
IN_VMEM = pl.BlockSpec(memory_space=pltpu.VMEM)
IN_HBM = pl.BlockSpec(memory_space=pltpu.HBM)
IN_SMEM = pl.BlockSpec(memory_space=pltpu.SMEM)


def params(limit=VMEM):
    return pltpu.CompilerParams(vmem_limit_bytes=limit)


def f32(*shape):
    return jax.ShapeDtypeStruct(shape, jnp.float32)


def whole(shape):
    return pl.BlockSpec(shape, lambda *_: (0,) * len(shape))


def cost(flops, nbytes):
    return pl.CostEstimate(flops=flops, bytes_accessed=nbytes, transcendentals=0)


def columns_of(rows):
    width = rows[0].shape[1]
    filled = jnp.concatenate(rows + [jnp.zeros((128 - len(rows), width), jnp.float32)], axis=0)
    if width < 128:
        filled = jnp.concatenate([filled, jnp.zeros((128, 128 - width), jnp.float32)], axis=1)
    turned = jnp.transpose(filled)
    return [turned[:T, i : i + 1] for i in range(len(rows))]


def score_kernel(q_hbm, w_ref, k_hbm, out_ref, by_head_ref, q_ref, k_ref, q_f32, sems):
    heads, tile, step = JL // 2, 512, 4
    k_copy = pltpu.make_async_copy(k_hbm, k_ref, sems.at[2])
    copies = [
        pltpu.make_async_copy(q_hbm.at[:, h * heads : (h + 1) * heads, :], q_ref.at[h], sems.at[h])
        for h in range(2)
    ]
    copies[0].start()
    k_copy.start()
    copies[1].start()
    w = columns_of([w_ref[j : j + 1, :] * SCALE for j in range(JL)])
    for h in range(2):
        copies[h].wait()
        q_f32[...] = q_ref[h].astype(jnp.float32).reshape(HALF, D)
        for j in range(heads):
            at = h * HALF + j * T
            by_head_ref[at : at + T, :] = q_f32[pl.ds(j, T, stride=heads), :].astype(jnp.bfloat16)
        if h == 0:
            k_copy.wait()
        for s in range(0, S, tile):
            acc = jnp.zeros((T, tile), jnp.float32) if h == 0 else out_ref[:, s : s + tile]
            for j0 in range(h * heads, (h + 1) * heads, step):
                logits = lax.dot_general(
                    by_head_ref[j0 * T : (j0 + step) * T, :],
                    k_ref[s : s + tile, :],
                    NT,
                    preferred_element_type=jnp.float32,
                )
                for j in range(step):
                    acc = acc + w[j0 + j] * jnp.maximum(logits[j * T : (j + 1) * T, :], 0.0)
            out_ref[:, s : s + tile] = acc


def score(q, w, k):
    return pl.pallas_call(
        score_kernel,
        in_specs=[IN_HBM, IN_VMEM, IN_HBM],
        out_specs=[IN_VMEM] * 2,
        out_shape=[f32(T, S), jax.ShapeDtypeStruct((ROWS, D), jnp.bfloat16)],
        scratch_shapes=[
            pltpu.VMEM((2, T, JL // 2, D), jnp.bfloat16),
            pltpu.VMEM((S, D), jnp.bfloat16),
            pltpu.VMEM((HALF, D), jnp.float32),
            pltpu.SemaphoreType.DMA((3,)),
        ],
        compiler_params=params(SCORE_VMEM),
        name="score",
    )(q, w, k)


def valid_mask(ctx):
    key = ctx * S + lax.broadcasted_iota(jnp.int32, (T, S), 1)
    query = POS + lax.broadcasted_iota(jnp.int32, (T, S), 0)
    return key <= query


def target_kernel(who_ref, target_ref, index_ref, w_ref, q_ref, normal_ref, sums_ref, held_ref, weighted_ref, payload_ref):
    held_ref[...] = index_ref[...]
    w = columns_of([w_ref[j : j + 1, :] for j in range(JL)])
    for j in range(JL):
        at = slice(j * T, (j + 1) * T)
        weighted_ref[at, :] = (q_ref[at, :].astype(jnp.float32) * w[j]).astype(jnp.bfloat16)
    core = who_ref[1]
    payload_ref[:HALF, :] = q_ref[pl.ds(pl.multiple_of(core * HALF, HALF), HALF), :].astype(jnp.float32)
    part = w_ref[pl.ds(pl.multiple_of(core * N_NEAR, N_NEAR), N_NEAR), :]
    payload_ref[HALF:, :] = jnp.concatenate([part, jnp.zeros((N_NEAR, 128 - T), jnp.float32)], axis=1)
    valid = valid_mask(who_ref[0])
    target = target_ref[...]
    masked = jnp.where(valid, target, 0.0)
    mass = jnp.sum(masked, axis=1, keepdims=True)
    entropy = jnp.sum(masked * jnp.log(target), axis=1, keepdims=True)
    normal_ref[...] = masked * (1.0 / mass)
    lane = lax.broadcasted_iota(jnp.int32, (T, 128), 1)
    sums_ref[...] = jnp.where(lane == 0, mass, entropy)


def target_sums(who, target, partial_index, w, q):
    return pl.pallas_call(
        target_kernel,
        in_specs=[IN_SMEM] + [IN_VMEM] * 4,
        out_specs=[IN_VMEM] * 5,
        out_shape=[
            f32(T, S),
            f32(T, 128),
            f32(T, S),
            jax.ShapeDtypeStruct((ROWS, D), jnp.bfloat16),
            f32(HALF + N_NEAR, D),
        ],
        compiler_params=params(),
        name="target",
    )(who, target, partial_index, w, q)


def stats_kernel(who_ref, mine_ref, other_ref, target_ref, sums_ref, index_ref, stats_ref, parts_ref):
    index = mine_ref[...] + other_ref[...]
    index_ref[...] = index
    valid = valid_mask(who_ref[0])
    target = target_ref[...]
    row_max = jnp.max(jnp.where(valid, index, -jnp.inf), axis=1, keepdims=True)
    expo = jnp.where(valid, jnp.exp(index - row_max), 0.0)
    denom = jnp.sum(expo, axis=1, keepdims=True)
    mass, entropy = sums_ref[:, 0:1], sums_ref[:, 1:2]
    cross = mass * jnp.sum(target * index, axis=1, keepdims=True)
    lane = lax.broadcasted_iota(jnp.int32, (T, 128), 1)
    packed = jnp.zeros((T, 128), jnp.float32)
    soft = expo * (1.0 / denom)
    peaks = (jnp.sum(x * x, axis=1, keepdims=True) for x in (soft, target))
    mixed = jnp.where(next(peaks) <= 4.0 * next(peaks), 1.0, 0.0)
    for i, column in enumerate((row_max, denom, mass, entropy, cross, mixed)):
        packed = jnp.where(lane == i, column, packed)
    packed = jnp.concatenate([packed, jnp.zeros((128 - T, 128), jnp.float32)], axis=0)
    stats_ref[...] = jnp.transpose(packed)[:8, :]
    parts_ref[0] = soft.astype(jnp.bfloat16)
    parts_ref[1] = (mixed * soft - target).astype(jnp.bfloat16)


def local_stats(who, mine, other, target, sums):
    return pl.pallas_call(
        stats_kernel,
        in_specs=[IN_SMEM] + [IN_VMEM] * 4,
        out_specs=[IN_VMEM] * 3,
        out_shape=[f32(T, S), f32(8, 128), jax.ShapeDtypeStruct((2, T, S), jnp.bfloat16)],
        compiler_params=params(),
        name="stats",
    )(who, mine, other, target, sums)


def query_kernel(who_ref, parts_ref, stats_ref, q_ref, k_ref, out_ref):
    block = 4 * T
    for r in range(0, HALF, block):
        at = pl.multiple_of(who_ref[0] * HALF + r, block)
        logits = lax.dot_general(
            q_ref[pl.ds(at, block), :], k_ref[...], NT, preferred_element_type=jnp.float32
        )
        positive = logits.astype(jnp.bfloat16) > 0.0
        for i in range(2):
            part = jnp.concatenate([parts_ref[i]] * (block // T), axis=0)
            picked = jnp.where(positive, part, jnp.zeros_like(part))
            at = slice(i * HALF + r, i * HALF + r + block)
            out_ref[at, :] = jnp.dot(picked, k_ref[...], preferred_element_type=jnp.float32)
    out_ref[ROWS:, :] = stats_ref[...]


def query_sums(half, parts, stats, q, k, name):
    return pl.pallas_call(
        query_kernel,
        in_specs=[IN_SMEM] + [IN_VMEM] * 4,
        out_specs=IN_VMEM,
        out_shape=f32(ROWS + 8, D),
        compiler_params=params(),
        cost_estimate=cost(6 * HALF * S * D, 4 << 20),
        name=name,
    )(half, parts, stats, q, k)


def merge(stats):
    row_max = stats[0][0:1]
    for s in stats[1:]:
        row_max = jnp.maximum(row_max, s[0:1])
    denom, rest = 0.0, 0.0
    for s in stats:
        denom = denom + s[1:2] * jnp.exp(s[0:1] - row_max)
        rest = rest + s[2:8]
    return jnp.concatenate([row_max, denom, rest], axis=0)


def shares(part, total):
    return part[1:2] * jnp.exp(part[0:1] - total[0:1]) / total[1:2], part[2:3] / total[2:3]


def pack_kernel(keep_ref, recv_ref, out_ref):
    mine, other = keep_ref[ROWS:, :], recv_ref[ROWS:, :]
    chip = merge([mine, other])
    rows = [*shares(mine, chip), mine[5:6], *shares(other, chip), other[5:6]]
    soft_a, target_a, mixed_a, soft_b, target_b, mixed_b = columns_of(rows)
    gap_a, gap_b = soft_a - mixed_a * target_a, soft_b - mixed_b * target_b
    for i in range(N_NEAR):
        at, too = slice(i * CHUNK, (i + 1) * CHUNK), slice(HALF + i * CHUNK, HALF + (i + 1) * CHUNK)
        a, b = keep_ref[at, :], recv_ref[at, :]
        out_ref[i, :CHUNK, :] = soft_a * a + soft_b * b
        gap = gap_a * a + gap_b * b + target_a * keep_ref[too, :] + target_b * recv_ref[too, :]
        out_ref[i, CHUNK : 2 * CHUNK, :] = gap
        out_ref[i, 2 * CHUNK :, :] = chip


def pack(keep, recv):
    return pl.pallas_call(
        pack_kernel,
        in_specs=[IN_VMEM] * 2,
        out_specs=IN_VMEM,
        out_shape=f32(N_NEAR, 2 * CHUNK + 8, 128),
        compiler_params=params(),
        name="pack",
    )(keep, recv)


def combine_parts(refs):
    parts = [ref[2 * CHUNK :, :] for ref in refs]
    total = merge(parts)
    columns = columns_of([row for part in parts for row in shares(part, total)])
    soft_sum, gap_sum = 0.0, 0.0
    for i, ref in enumerate(refs):
        soft, target = columns[2 * i], columns[2 * i + 1]
        a = ref[:CHUNK, :]
        soft_sum = soft_sum + soft * a
        gap_sum = gap_sum + (soft - target) * a + target * ref[CHUNK : 2 * CHUNK, :]
    return total, soft_sum, gap_sum


def near_kernel(in_ref, out_ref):
    total, soft_sum, gap_sum = combine_parts([in_ref.at[i] for i in range(N_NEAR)])
    out_ref[:CHUNK, :] = soft_sum
    out_ref[CHUNK : 2 * CHUNK, :] = gap_sum
    out_ref[2 * CHUNK :, :] = total


def combine_near(received):
    return pl.pallas_call(
        near_kernel,
        in_specs=[IN_VMEM],
        out_specs=IN_VMEM,
        out_shape=f32(2 * CHUNK + 8, D),
        compiler_params=params(),
        name="combine_near",
    )(received)


def far_kernel(who_ref, a_ref, b_ref, c_ref, d_ref, w_ref, q_ref, out_ref, stats_ref, loss_ref):
    total, _, gap_sum = combine_parts([a_ref, b_ref, c_ref, d_ref])
    row_max, denom, mass, entropy, cross = (total[i : i + 1] for i in range(5))
    stats_ref[...] = total
    loss = entropy / mass - jnp.log(mass) - cross / mass + row_max + jnp.log(denom)
    loss_ref[...] = loss[0, :T]
    gap_sum = gap_sum * (SCALE / T)
    head = who_ref[2]
    scaled = gap_sum * columns_of([w_ref[pl.ds(head, 1), :]])[0]
    q = q_ref[pl.ds(pl.multiple_of(head * T, T), T), :].astype(jnp.float32)
    grads = jnp.broadcast_to(jnp.sum(gap_sum * q, axis=1, keepdims=True), (T, 128))
    grads = jnp.transpose(jnp.concatenate([grads, grads], axis=0))[:8]
    for p in range(N_NEAR):
        out_ref[p, :CHUNK, :] = scaled
        out_ref[p, CHUNK:, :] = grads


def combine_far(who, own, far, w, q):
    return pl.pallas_call(
        far_kernel,
        in_specs=[IN_SMEM] + [IN_VMEM] * 6,
        out_specs=[IN_VMEM] * 3,
        out_shape=[f32(N_NEAR, CHUNK + 8, D), f32(8, 128), f32(T)],
        compiler_params=params(),
        name="combine_far",
    )(who, own, *far, w, q)


def place_half(half, at, out_hbm, sem):
    copies = []
    for p in range(N_NEAR):
        ref, i = at(p)
        to = out_hbm.at[:, half * N_NEAR + p, :]
        copies.append(pltpu.make_async_copy(ref.at[i, :CHUNK, :], to, sem.at[p]))
    for copy in copies:
        copy.start()
    return copies


def first_kernel(who_ref, mine_ref, out_hbm, sem):
    for copy in place_half(who_ref[1], lambda p: (mine_ref, p), out_hbm, sem):
        copy.wait()


def last_kernel(who_ref, mine_ref, lower_ref, upper_ref, begun_hbm, out_hbm, weights_hbm, sem, weights_ref, weights_sem):
    def mine_at(p):
        return mine_ref, p

    def other_at(p):
        return (lower_ref, p) if p < N_NEAR // 2 else (upper_ref, p - N_NEAR // 2)

    copies = place_half(1 - who_ref[1], other_at, out_hbm, sem)

    def emit(first, second):
        for half, at in enumerate((first, second)):
            for p in range(N_NEAR):
                ref, i = at(p)
                row = half * N_NEAR + p
                weights_ref[row : row + 1, :] = ref[i, CHUNK : CHUNK + 1, :T]

    pl.when(who_ref[1] == 0)(lambda: emit(mine_at, other_at))
    pl.when(who_ref[1] == 1)(lambda: emit(other_at, mine_at))
    copies.append(pltpu.make_async_copy(weights_ref, weights_hbm, weights_sem))
    copies[-1].start()
    for copy in copies:
        copy.wait()


HALF_SCRATCH = [pltpu.SemaphoreType.DMA((N_NEAR,))]


def place_mine(who, mine):
    return pl.pallas_call(
        first_kernel,
        in_specs=[IN_SMEM, IN_VMEM],
        out_specs=IN_HBM,
        out_shape=f32(T, JL, D),
        scratch_shapes=HALF_SCRATCH,
        compiler_params=params(),
        name="place_mine",
    )(who, mine)


def place_other(who, mine, other, begun):
    return pl.pallas_call(
        last_kernel,
        in_specs=[IN_SMEM, IN_VMEM, IN_VMEM, IN_VMEM, IN_HBM],
        out_specs=[IN_HBM] * 2,
        out_shape=[f32(T, JL, D), f32(JL, T)],
        scratch_shapes=HALF_SCRATCH + [pltpu.VMEM((JL, T), jnp.float32), pltpu.SemaphoreType.DMA(())],
        input_output_aliases={4: 0},
        compiler_params=params(),
        name="place_other",
    )(who, mine, *other, begun)


def unpack_kernel(payload_ref, q_ref, weighted_ref):
    w = columns_of([payload_ref[HALF + j : HALF + j + 1, :] for j in range(N_NEAR)])
    for j in range(N_NEAR):
        at = slice(j * T, (j + 1) * T)
        q = payload_ref[at, :]
        q_ref[at, :] = q.astype(jnp.bfloat16)
        weighted_ref[at, :] = (q * w[j]).astype(jnp.bfloat16)


KEY_TILE = 256


def key_sums(gap, k, q_ref, weighted_ref):
    span = 1024
    gap = jnp.concatenate([gap] * (span // 128), axis=1)
    acc = jnp.zeros((KEY_TILE, D), jnp.float32)
    for r in range(0, q_ref.shape[0], span):
        logits = lax.dot_general(k, q_ref[r : r + span, :], NT, preferred_element_type=jnp.float32)
        picked = jnp.where(logits > 0.0, gap, 0.0).astype(jnp.bfloat16)
        acc = acc + jnp.dot(picked, weighted_ref[r : r + span, :], preferred_element_type=jnp.float32)
    return acc


def own_kernel(who_ref, index_ref, target_ref, stats_ref, q_ref, weighted_ref, k_ref, out_ref, gap_ref):
    row_max, denom, mass = columns_of([stats_ref[i : i + 1, :] for i in range(3)])
    gap = jnp.exp(index_ref[...] - row_max) * (1.0 / denom) - target_ref[...] * (1.0 / mass)
    gap = jnp.where(valid_mask(who_ref[0]), gap, 0.0) * (SCALE / T)
    for s in range(0, S, KEY_TILE):
        at = slice(s, s + KEY_TILE)
        turned = jnp.transpose(jnp.concatenate([gap[:, at]] * 2, axis=0))
        gap_ref[at, :] = turned
        out_ref[at, :] = key_sums(turned, k_ref[at, :], q_ref, weighted_ref)


def own_key_grads(who, index, target, stats, q, weighted, k):
    return pl.pallas_call(
        own_kernel,
        in_specs=[IN_SMEM] + [IN_VMEM] * 6,
        out_specs=[IN_VMEM] * 2,
        out_shape=[f32(S, D)] * 2,
        compiler_params=params(),
        cost_estimate=cost(4 * ROWS * S * D, 4 << 20),
        name="own_key_grads",
    )(who, index, target, stats, q, weighted, k)


def other_kernel(
    own_ref, gap_ref, k_ref, payload_a_ref, payload_b_ref, out_hbm,
    q_a_ref, weighted_a_ref, q_b_ref, weighted_b_ref, out_ref, sems,
):
    unpack_kernel(payload_a_ref, q_a_ref, weighted_a_ref)
    unpack_kernel(payload_b_ref, q_b_ref, weighted_b_ref)
    copies = []
    for s in range(0, S, KEY_TILE):
        at = slice(s, s + KEY_TILE)
        gap, k = gap_ref[at, :], k_ref[at, :]
        both = key_sums(gap, k, q_a_ref, weighted_a_ref) + key_sums(gap, k, q_b_ref, weighted_b_ref)
        out_ref[at, :] = own_ref[at, :] + both
        copies.append(pltpu.make_async_copy(out_ref.at[at], out_hbm.at[at], sems.at[s // KEY_TILE]))
        copies[-1].start()
    for copy in copies:
        copy.wait()


def key_grads(own, gap, k, *heads):
    return pl.pallas_call(
        other_kernel,
        in_specs=[IN_VMEM] * 5,
        out_specs=IN_HBM,
        out_shape=f32(S, D),
        scratch_shapes=[pltpu.VMEM((HALF, D), jnp.bfloat16)] * 4
        + [pltpu.VMEM((S, D), jnp.float32), pltpu.SemaphoreType.DMA((S // KEY_TILE,))],
        compiler_params=params(),
        cost_estimate=cost(4 * ROWS * S * D, 4 << 20),
        name="key_grads",
    )(own, gap, k, *heads)


def on_device(index_queries, head_weights, index_keys, main_target):
    swap = [(0, 1), (1, 0)]
    core = lax.axis_index("c")
    head = core * N_NEAR + lax.axis_index(NEAR)
    who = jnp.stack([lax.axis_index(CTX), core, head]).astype(jnp.int32)
    w = head_weights.T
    partial_index, q = score(index_queries, w, index_keys)
    other_index = lax.ppermute(partial_index, "yh", swap)
    target, target_sum, held_index, weighted, payload = target_sums(who, main_target, partial_index, w, q)
    payload = lax.ppermute(payload, "yh", swap)
    payloads = [payload, lax.ppermute(payload, "c", swap)]
    index, stats, parts = local_stats(who, held_index, other_index, target, target_sum)

    send = query_sums(1 - who[1:2], parts, stats, q, index_keys, "query_sums_send")
    recv = lax.ppermute(send, "c", swap)
    keep = query_sums(who[1:2], parts, stats, q, index_keys, "query_sums_keep")
    near = lax.all_to_all(pack(keep, recv), NEAR, 0, 0, tiled=True)
    own = combine_near(near)
    far = [lax.ppermute(own, FAR, [(i, i ^ d) for i in range(N_FAR)]) for d in range(1, N_FAR)]
    chunk, total_stats, loss = combine_far(who, own, far, w, q)

    mine = lax.all_to_all(chunk, NEAR, 0, 0, tiled=True)
    own, gap = own_key_grads(who, index, main_target, total_stats, q, weighted, index_keys)
    grad_keys = key_grads(own, gap, index_keys, *payloads)
    mine, grad_keys = lax.optimization_barrier((mine, grad_keys))
    half = N_NEAR // 2
    other = [lax.ppermute(x, "c", swap) for x in (mine[:half], mine[half:])]
    grad_queries, grad_weights = place_other(who, mine, other, place_mine(who, mine))
    return grad_queries, grad_weights.T, grad_keys, loss


def solution(mesh):
    fine = Mesh(mesh.devices.reshape(N_FAR, 2, 2, 4, 2, 2), CTX + ("yh",))
    return jax.shard_map(
        on_device,
        mesh=fine,
        in_specs=(P(None, "yh", None), P(None, "yh"), P(CTX, None), P(None, CTX)),
        out_specs=(P(None, "yh", None), P(None, "yh"), P(CTX, None), P()),
        check_vma=False,
    )
```

```python
import jax
import jax.numpy as jnp
from jax import lax
from jax.experimental import pallas as pl
from jax.experimental.pallas import tpu as pltpu
from jax.sharding import Mesh, PartitionSpec as P

H = 64
T = 64
JL = 32
D = 128
S = 1024
ROWS = T * JL
HALF = ROWS // 2
POS = 131072 - T
SCALE = (D**-0.5) * (H**-0.5)
CTX = ("zh", "zl", "yl", "x", "c")
NEAR = ("x", "yl", "zl")
FAR = "zh"
N_NEAR = 16
N_FAR = 4
CHUNK = HALF // N_NEAR
KEY_ROWS = S
VMEM = 48 * 1024 * 1024
SCORE_VMEM = 60 * 1024 * 1024
NT = (((1,), (1,)), ((), ()))
IN_VMEM = pl.BlockSpec(memory_space=pltpu.VMEM)
IN_HBM = pl.BlockSpec(memory_space=pltpu.HBM)
IN_SMEM = pl.BlockSpec(memory_space=pltpu.SMEM)


def params(limit=VMEM):
    return pltpu.CompilerParams(vmem_limit_bytes=limit)


def f32(*shape):
    return jax.ShapeDtypeStruct(shape, jnp.float32)


def whole(shape):
    return pl.BlockSpec(shape, lambda *_: (0,) * len(shape))


def cost(flops, nbytes):
    return pl.CostEstimate(flops=flops, bytes_accessed=nbytes, transcendentals=0)


def columns_of(rows):
    width = rows[0].shape[1]
    filled = jnp.concatenate(rows + [jnp.zeros((128 - len(rows), width), jnp.float32)], axis=0)
    if width < 128:
        filled = jnp.concatenate([filled, jnp.zeros((128, 128 - width), jnp.float32)], axis=1)
    turned = jnp.transpose(filled)
    return [turned[:T, i : i + 1] for i in range(len(rows))]


def score_kernel(q_hbm, w_ref, k_hbm, out_ref, by_head_ref, q_ref, k_ref, q_f32, sems):
    heads, tile, step = JL // 2, 512, 4
    k_copy = pltpu.make_async_copy(k_hbm, k_ref, sems.at[2])
    copies = [
        pltpu.make_async_copy(q_hbm.at[:, h * heads : (h + 1) * heads, :], q_ref.at[h], sems.at[h])
        for h in range(2)
    ]
    copies[0].start()
    k_copy.start()
    copies[1].start()
    w = columns_of([w_ref[j : j + 1, :] * SCALE for j in range(JL)])
    for h in range(2):
        copies[h].wait()
        q_f32[...] = q_ref[h].astype(jnp.float32).reshape(HALF, D)
        for j in range(heads):
            at = h * HALF + j * T
            by_head_ref[at : at + T, :] = q_f32[pl.ds(j, T, stride=heads), :].astype(jnp.bfloat16)
        if h == 0:
            k_copy.wait()
        for s in range(0, S, tile):
            acc = jnp.zeros((T, tile), jnp.float32) if h == 0 else out_ref[:, s : s + tile]
            for j0 in range(h * heads, (h + 1) * heads, step):
                logits = lax.dot_general(
                    by_head_ref[j0 * T : (j0 + step) * T, :],
                    k_ref[s : s + tile, :],
                    NT,
                    preferred_element_type=jnp.float32,
                )
                for j in range(step):
                    acc = acc + w[j0 + j] * jnp.maximum(logits[j * T : (j + 1) * T, :], 0.0)
            out_ref[:, s : s + tile] = acc


def score(q, w, k):
    return pl.pallas_call(
        score_kernel,
        in_specs=[IN_HBM, IN_VMEM, IN_HBM],
        out_specs=[IN_VMEM] * 2,
        out_shape=[f32(T, S), jax.ShapeDtypeStruct((ROWS, D), jnp.bfloat16)],
        scratch_shapes=[
            pltpu.VMEM((2, T, JL // 2, D), jnp.bfloat16),
            pltpu.VMEM((S, D), jnp.bfloat16),
            pltpu.VMEM((HALF, D), jnp.float32),
            pltpu.SemaphoreType.DMA((3,)),
        ],
        compiler_params=params(SCORE_VMEM),
        name="score",
    )(q, w, k)


def valid_mask(ctx):
    key = ctx * S + lax.broadcasted_iota(jnp.int32, (T, S), 1)
    query = POS + lax.broadcasted_iota(jnp.int32, (T, S), 0)
    return key <= query


def target_kernel(who_ref, target_ref, index_ref, w_ref, q_ref, normal_ref, sums_ref, held_ref, weighted_ref, payload_ref):
    held_ref[...] = index_ref[...]
    w = columns_of([w_ref[j : j + 1, :] for j in range(JL)])
    for j in range(JL):
        at = slice(j * T, (j + 1) * T)
        weighted_ref[at, :] = (q_ref[at, :].astype(jnp.float32) * w[j]).astype(jnp.bfloat16)
    core = who_ref[1]
    payload_ref[:HALF, :] = q_ref[pl.ds(pl.multiple_of(core * HALF, HALF), HALF), :].astype(jnp.float32)
    part = w_ref[pl.ds(pl.multiple_of(core * N_NEAR, N_NEAR), N_NEAR), :]
    payload_ref[HALF:, :] = jnp.concatenate([part, jnp.zeros((N_NEAR, 128 - T), jnp.float32)], axis=1)
    valid = valid_mask(who_ref[0])
    target = target_ref[...]
    masked = jnp.where(valid, target, 0.0)
    mass = jnp.sum(masked, axis=1, keepdims=True)
    entropy = jnp.sum(masked * jnp.log(target), axis=1, keepdims=True)
    normal_ref[...] = masked * (1.0 / mass)
    lane = lax.broadcasted_iota(jnp.int32, (T, 128), 1)
    sums_ref[...] = jnp.where(lane == 0, mass, entropy)


def target_sums(who, target, partial_index, w, q):
    return pl.pallas_call(
        target_kernel,
        in_specs=[IN_SMEM] + [IN_VMEM] * 4,
        out_specs=[IN_VMEM] * 5,
        out_shape=[
            f32(T, S),
            f32(T, 128),
            f32(T, S),
            jax.ShapeDtypeStruct((ROWS, D), jnp.bfloat16),
            f32(HALF + N_NEAR, D),
        ],
        compiler_params=params(),
        name="target",
    )(who, target, partial_index, w, q)


def stats_kernel(who_ref, mine_ref, other_ref, target_ref, sums_ref, index_ref, stats_ref, parts_ref):
    index = mine_ref[...] + other_ref[...]
    index_ref[...] = index
    valid = valid_mask(who_ref[0])
    target = target_ref[...]
    row_max = jnp.max(jnp.where(valid, index, -jnp.inf), axis=1, keepdims=True)
    expo = jnp.where(valid, jnp.exp(index - row_max), 0.0)
    denom = jnp.sum(expo, axis=1, keepdims=True)
    mass, entropy = sums_ref[:, 0:1], sums_ref[:, 1:2]
    cross = mass * jnp.sum(target * index, axis=1, keepdims=True)
    lane = lax.broadcasted_iota(jnp.int32, (T, 128), 1)
    packed = jnp.zeros((T, 128), jnp.float32)
    soft = expo * (1.0 / denom)
    peaks = (jnp.sum(x * x, axis=1, keepdims=True) for x in (soft, target))
    mixed = jnp.where(next(peaks) <= 4.0 * next(peaks), 1.0, 0.0)
    for i, column in enumerate((row_max, denom, mass, entropy, cross, mixed)):
        packed = jnp.where(lane == i, column, packed)
    packed = jnp.concatenate([packed, jnp.zeros((128 - T, 128), jnp.float32)], axis=0)
    stats_ref[...] = jnp.transpose(packed)[:8, :]
    parts_ref[0] = soft.astype(jnp.bfloat16)
    parts_ref[1] = (mixed * soft - target).astype(jnp.bfloat16)


def local_stats(who, mine, other, target, sums):
    return pl.pallas_call(
        stats_kernel,
        in_specs=[IN_SMEM] + [IN_VMEM] * 4,
        out_specs=[IN_VMEM] * 3,
        out_shape=[f32(T, S), f32(8, 128), jax.ShapeDtypeStruct((2, T, S), jnp.bfloat16)],
        compiler_params=params(),
        name="stats",
    )(who, mine, other, target, sums)


def query_kernel(who_ref, parts_ref, stats_ref, q_ref, k_ref, out_ref):
    block = 4 * T
    for r in range(0, HALF, block):
        at = pl.multiple_of(who_ref[0] * HALF + r, block)
        logits = lax.dot_general(
            q_ref[pl.ds(at, block), :], k_ref[...], NT, preferred_element_type=jnp.float32
        )
        positive = logits.astype(jnp.bfloat16) > 0.0
        for i in range(2):
            part = jnp.concatenate([parts_ref[i]] * (block // T), axis=0)
            picked = jnp.where(positive, part, jnp.zeros_like(part))
            at = slice(i * HALF + r, i * HALF + r + block)
            out_ref[at, :] = jnp.dot(picked, k_ref[...], preferred_element_type=jnp.float32)
    out_ref[ROWS:, :] = stats_ref[...]


def query_sums(half, parts, stats, q, k, name):
    return pl.pallas_call(
        query_kernel,
        in_specs=[IN_SMEM] + [IN_VMEM] * 4,
        out_specs=IN_VMEM,
        out_shape=f32(ROWS + 8, D),
        compiler_params=params(),
        cost_estimate=cost(6 * HALF * S * D, 4 << 20),
        name=name,
    )(half, parts, stats, q, k)


def merge(stats):
    row_max = stats[0][0:1]
    for s in stats[1:]:
        row_max = jnp.maximum(row_max, s[0:1])
    denom, rest = 0.0, 0.0
    for s in stats:
        denom = denom + s[1:2] * jnp.exp(s[0:1] - row_max)
        rest = rest + s[2:8]
    return jnp.concatenate([row_max, denom, rest], axis=0)


def shares(part, total):
    return part[1:2] * jnp.exp(part[0:1] - total[0:1]) / total[1:2], part[2:3] / total[2:3]


def pack_kernel(keep_ref, recv_ref, out_ref):
    mine, other = keep_ref[ROWS:, :], recv_ref[ROWS:, :]
    chip = merge([mine, other])
    rows = [*shares(mine, chip), mine[5:6], *shares(other, chip), other[5:6]]
    soft_a, target_a, mixed_a, soft_b, target_b, mixed_b = columns_of(rows)
    gap_a, gap_b = soft_a - mixed_a * target_a, soft_b - mixed_b * target_b
    for i in range(N_NEAR):
        at, too = slice(i * CHUNK, (i + 1) * CHUNK), slice(HALF + i * CHUNK, HALF + (i + 1) * CHUNK)
        a, b = keep_ref[at, :], recv_ref[at, :]
        out_ref[i, :CHUNK, :] = soft_a * a + soft_b * b
        gap = gap_a * a + gap_b * b + target_a * keep_ref[too, :] + target_b * recv_ref[too, :]
        out_ref[i, CHUNK : 2 * CHUNK, :] = gap
        out_ref[i, 2 * CHUNK :, :] = chip


def pack(keep, recv):
    return pl.pallas_call(
        pack_kernel,
        in_specs=[IN_VMEM] * 2,
        out_specs=IN_VMEM,
        out_shape=f32(N_NEAR, 2 * CHUNK + 8, 128),
        compiler_params=params(),
        name="pack",
    )(keep, recv)


def combine_parts(refs):
    parts = [ref[2 * CHUNK :, :] for ref in refs]
    total = merge(parts)
    columns = columns_of([row for part in parts for row in shares(part, total)])
    soft_sum, gap_sum = 0.0, 0.0
    for i, ref in enumerate(refs):
        soft, target = columns[2 * i], columns[2 * i + 1]
        a = ref[:CHUNK, :]
        soft_sum = soft_sum + soft * a
        gap_sum = gap_sum + (soft - target) * a + target * ref[CHUNK : 2 * CHUNK, :]
    return total, soft_sum, gap_sum


def near_kernel(in_ref, out_ref):
    total, soft_sum, gap_sum = combine_parts([in_ref.at[i] for i in range(N_NEAR)])
    out_ref[:CHUNK, :] = soft_sum
    out_ref[CHUNK : 2 * CHUNK, :] = gap_sum
    out_ref[2 * CHUNK :, :] = total


def combine_near(received):
    return pl.pallas_call(
        near_kernel,
        in_specs=[IN_VMEM],
        out_specs=IN_VMEM,
        out_shape=f32(2 * CHUNK + 8, D),
        compiler_params=params(),
        name="combine_near",
    )(received)


def far_kernel(who_ref, a_ref, b_ref, c_ref, d_ref, w_ref, q_ref, out_ref, stats_ref, loss_ref):
    total, _, gap_sum = combine_parts([a_ref, b_ref, c_ref, d_ref])
    row_max, denom, mass, entropy, cross = (total[i : i + 1] for i in range(5))
    stats_ref[...] = total
    loss = entropy / mass - jnp.log(mass) - cross / mass + row_max + jnp.log(denom)
    loss_ref[...] = loss[0, :T]
    gap_sum = gap_sum * (SCALE / T)
    head = who_ref[2]
    scaled = gap_sum * columns_of([w_ref[pl.ds(head, 1), :]])[0]
    q = q_ref[pl.ds(pl.multiple_of(head * T, T), T), :].astype(jnp.float32)
    grads = jnp.broadcast_to(jnp.sum(gap_sum * q, axis=1, keepdims=True), (T, 128))
    grads = jnp.transpose(jnp.concatenate([grads, grads], axis=0))[:8]
    for p in range(N_NEAR):
        out_ref[p, :CHUNK, :] = scaled
        out_ref[p, CHUNK:, :] = grads


def combine_far(who, own, far, w, q):
    return pl.pallas_call(
        far_kernel,
        in_specs=[IN_SMEM] + [IN_VMEM] * 6,
        out_specs=[IN_VMEM] * 3,
        out_shape=[f32(N_NEAR, CHUNK + 8, D), f32(8, 128), f32(T)],
        compiler_params=params(),
        name="combine_far",
    )(who, own, *far, w, q)


def place_half(half, at, out_hbm, sem):
    copies = []
    for p in range(N_NEAR):
        ref, i = at(p)
        to = out_hbm.at[:, half * N_NEAR + p, :]
        copies.append(pltpu.make_async_copy(ref.at[i, :CHUNK, :], to, sem.at[p]))
    for copy in copies:
        copy.start()
    return copies


def first_kernel(who_ref, mine_ref, out_hbm, sem):
    for copy in place_half(who_ref[1], lambda p: (mine_ref, p), out_hbm, sem):
        copy.wait()


def last_kernel(who_ref, mine_ref, other_ref, begun_hbm, out_hbm, weights_hbm, sem, weights_ref, weights_sem):
    def mine_at(p):
        return mine_ref, p

    def other_at(p):
        return other_ref, p

    copies = place_half(1 - who_ref[1], other_at, out_hbm, sem)

    def emit(first, second):
        for half, at in enumerate((first, second)):
            for p in range(N_NEAR):
                ref, i = at(p)
                row = half * N_NEAR + p
                weights_ref[row : row + 1, :] = ref[i, CHUNK : CHUNK + 1, :T]

    pl.when(who_ref[1] == 0)(lambda: emit(mine_at, other_at))
    pl.when(who_ref[1] == 1)(lambda: emit(other_at, mine_at))
    copies.append(pltpu.make_async_copy(weights_ref, weights_hbm, weights_sem))
    copies[-1].start()
    for copy in copies:
        copy.wait()


HALF_SCRATCH = [pltpu.SemaphoreType.DMA((N_NEAR,))]


def place_mine(who, mine):
    return pl.pallas_call(
        first_kernel,
        in_specs=[IN_SMEM, IN_VMEM],
        out_specs=IN_HBM,
        out_shape=f32(T, JL, D),
        scratch_shapes=HALF_SCRATCH,
        compiler_params=params(),
        name="place_mine",
    )(who, mine)


def place_other(who, mine, other, begun):
    return pl.pallas_call(
        last_kernel,
        in_specs=[IN_SMEM, IN_VMEM, IN_VMEM, IN_HBM],
        out_specs=[IN_HBM] * 2,
        out_shape=[f32(T, JL, D), f32(JL, T)],
        scratch_shapes=HALF_SCRATCH + [pltpu.VMEM((JL, T), jnp.float32), pltpu.SemaphoreType.DMA(())],
        input_output_aliases={3: 0},
        compiler_params=params(),
        name="place_other",
    )(who, mine, *other, begun)


def unpack_kernel(payload_ref, q_ref, weighted_ref):
    w = columns_of([payload_ref[HALF + j : HALF + j + 1, :] for j in range(N_NEAR)])
    for j in range(N_NEAR):
        at = slice(j * T, (j + 1) * T)
        q = payload_ref[at, :]
        q_ref[at, :] = q.astype(jnp.bfloat16)
        weighted_ref[at, :] = (q * w[j]).astype(jnp.bfloat16)


KEY_TILE = 256


def key_sums(gap, k, q_ref, weighted_ref):
    span = 1024
    gap = jnp.concatenate([gap] * (span // 128), axis=1)
    acc = jnp.zeros((KEY_TILE, D), jnp.float32)
    for r in range(0, q_ref.shape[0], span):
        logits = lax.dot_general(k, q_ref[r : r + span, :], NT, preferred_element_type=jnp.float32)
        picked = jnp.where(logits > 0.0, gap, 0.0).astype(jnp.bfloat16)
        acc = acc + jnp.dot(picked, weighted_ref[r : r + span, :], preferred_element_type=jnp.float32)
    return acc


def own_kernel(who_ref, index_ref, target_ref, stats_ref, q_ref, weighted_ref, k_ref, out_ref, gap_ref):
    row_max, denom, mass = columns_of([stats_ref[i : i + 1, :] for i in range(3)])
    gap = jnp.exp(index_ref[...] - row_max) * (1.0 / denom) - target_ref[...] * (1.0 / mass)
    gap = jnp.where(valid_mask(who_ref[0]), gap, 0.0) * (SCALE / T)
    for s in range(0, S, KEY_TILE):
        at = slice(s, s + KEY_TILE)
        turned = jnp.transpose(jnp.concatenate([gap[:, at]] * 2, axis=0))
        gap_ref[at, :] = turned
        out_ref[at, :] = key_sums(turned, k_ref[at, :], q_ref, weighted_ref)


def own_key_grads(who, index, target, stats, q, weighted, k):
    return pl.pallas_call(
        own_kernel,
        in_specs=[IN_SMEM] + [IN_VMEM] * 6,
        out_specs=[IN_VMEM] * 2,
        out_shape=[f32(S, D)] * 2,
        compiler_params=params(),
        cost_estimate=cost(4 * ROWS * S * D, 4 << 20),
        name="own_key_grads",
    )(who, index, target, stats, q, weighted, k)


def other_kernel(
    own_ref, gap_ref, k_ref, payload_a_ref, payload_b_ref, out_hbm,
    q_a_ref, weighted_a_ref, q_b_ref, weighted_b_ref, out_ref, sems,
):
    unpack_kernel(payload_a_ref, q_a_ref, weighted_a_ref)
    unpack_kernel(payload_b_ref, q_b_ref, weighted_b_ref)
    copies = []
    for s in range(0, S, KEY_TILE):
        at = slice(s, s + KEY_TILE)
        gap, k = gap_ref[at, :], k_ref[at, :]
        both = key_sums(gap, k, q_a_ref, weighted_a_ref) + key_sums(gap, k, q_b_ref, weighted_b_ref)
        out_ref[at, :] = own_ref[at, :] + both
        copies.append(pltpu.make_async_copy(out_ref.at[at], out_hbm.at[at], sems.at[s // KEY_TILE]))
        copies[-1].start()
    for copy in copies:
        copy.wait()


def key_grads(own, gap, k, *heads):
    return pl.pallas_call(
        other_kernel,
        in_specs=[IN_VMEM] * 5,
        out_specs=IN_HBM,
        out_shape=f32(S, D),
        scratch_shapes=[pltpu.VMEM((HALF, D), jnp.bfloat16)] * 4
        + [pltpu.VMEM((S, D), jnp.float32), pltpu.SemaphoreType.DMA((S // KEY_TILE,))],
        compiler_params=params(),
        cost_estimate=cost(4 * ROWS * S * D, 4 << 20),
        name="key_grads",
    )(own, gap, k, *heads)


def on_device(index_queries, head_weights, index_keys, main_target):
    swap = [(0, 1), (1, 0)]
    core = lax.axis_index("c")
    head = core * N_NEAR + lax.axis_index(NEAR)
    who = jnp.stack([lax.axis_index(CTX), core, head]).astype(jnp.int32)
    w = head_weights.T
    partial_index, q = score(index_queries, w, index_keys)
    other_index = lax.ppermute(partial_index, "yh", swap)
    target, target_sum, held_index, weighted, payload = target_sums(who, main_target, partial_index, w, q)
    payload = lax.ppermute(payload, "yh", swap)
    payloads = [payload, lax.ppermute(payload, "c", swap)]
    index, stats, parts = local_stats(who, held_index, other_index, target, target_sum)

    send = query_sums(1 - who[1:2], parts, stats, q, index_keys, "query_sums_send")
    recv = lax.ppermute(send, "c", swap)
    keep = query_sums(who[1:2], parts, stats, q, index_keys, "query_sums_keep")
    near = lax.all_to_all(pack(keep, recv), NEAR, 0, 0, tiled=True)
    own = combine_near(near)
    far = [lax.ppermute(own, FAR, [(i, i ^ d) for i in range(N_FAR)]) for d in range(1, N_FAR)]
    chunk, total_stats, loss = combine_far(who, own, far, w, q)

    mine = lax.all_to_all(chunk, NEAR, 0, 0, tiled=True)
    own, gap = own_key_grads(who, index, main_target, total_stats, q, weighted, index_keys)
    grad_keys = key_grads(own, gap, index_keys, *payloads)
    mine, grad_keys = lax.optimization_barrier((mine, grad_keys))
    other = [lax.ppermute(mine, "c", swap)]
    grad_queries, grad_weights = place_other(who, mine, other, place_mine(who, mine))
    return grad_queries, grad_weights.T, grad_keys, loss


def solution(mesh):
    fine = Mesh(mesh.devices.reshape(N_FAR, 2, 2, 4, 2, 2), CTX + ("yh",))
    return jax.shard_map(
        on_device,
        mesh=fine,
        in_specs=(P(None, "yh", None), P(None, "yh"), P(CTX, None), P(None, CTX)),
        out_specs=(P(None, "yh", None), P(None, "yh"), P(CTX, None), P()),
        check_vma=False,
    )
```

```python
import jax
import jax.numpy as jnp
from jax import lax
from jax.experimental import pallas as pl
from jax.experimental.pallas import tpu as pltpu
from jax.sharding import Mesh, PartitionSpec as P

H = 64
T = 64
JL = 32
D = 128
S = 1024
ROWS = T * JL
HALF = ROWS // 2
POS = 131072 - T
SCALE = (D**-0.5) * (H**-0.5)
CTX = ("zh", "zl", "yl", "x", "c")
NEAR = ("x", "zl", "yl")
FAR = "zh"
N_NEAR = 16
N_FAR = 4
CHUNK = HALF // N_NEAR
KEY_ROWS = S
VMEM = 48 * 1024 * 1024
SCORE_VMEM = 60 * 1024 * 1024
NT = (((1,), (1,)), ((), ()))
IN_VMEM = pl.BlockSpec(memory_space=pltpu.VMEM)
IN_HBM = pl.BlockSpec(memory_space=pltpu.HBM)
IN_SMEM = pl.BlockSpec(memory_space=pltpu.SMEM)


def params(limit=VMEM):
    return pltpu.CompilerParams(vmem_limit_bytes=limit)


def f32(*shape):
    return jax.ShapeDtypeStruct(shape, jnp.float32)


def whole(shape):
    return pl.BlockSpec(shape, lambda *_: (0,) * len(shape))


def cost(flops, nbytes):
    return pl.CostEstimate(flops=flops, bytes_accessed=nbytes, transcendentals=0)


def columns_of(rows):
    width = rows[0].shape[1]
    filled = jnp.concatenate(rows + [jnp.zeros((128 - len(rows), width), jnp.float32)], axis=0)
    if width < 128:
        filled = jnp.concatenate([filled, jnp.zeros((128, 128 - width), jnp.float32)], axis=1)
    turned = jnp.transpose(filled)
    return [turned[:T, i : i + 1] for i in range(len(rows))]


def score_kernel(q_hbm, w_ref, k_hbm, out_ref, by_head_ref, q_ref, k_ref, q_f32, sems):
    heads, tile, step = JL // 2, 512, 4
    k_copy = pltpu.make_async_copy(k_hbm, k_ref, sems.at[2])
    copies = [
        pltpu.make_async_copy(q_hbm.at[:, h * heads : (h + 1) * heads, :], q_ref.at[h], sems.at[h])
        for h in range(2)
    ]
    copies[0].start()
    k_copy.start()
    copies[1].start()
    w = columns_of([w_ref[j : j + 1, :] * SCALE for j in range(JL)])
    for h in range(2):
        copies[h].wait()
        q_f32[...] = q_ref[h].astype(jnp.float32).reshape(HALF, D)
        for j in range(heads):
            at = h * HALF + j * T
            by_head_ref[at : at + T, :] = q_f32[pl.ds(j, T, stride=heads), :].astype(jnp.bfloat16)
        if h == 0:
            k_copy.wait()
        for s in range(0, S, tile):
            acc = jnp.zeros((T, tile), jnp.float32) if h == 0 else out_ref[:, s : s + tile]
            for j0 in range(h * heads, (h + 1) * heads, step):
                logits = lax.dot_general(
                    by_head_ref[j0 * T : (j0 + step) * T, :],
                    k_ref[s : s + tile, :],
                    NT,
                    preferred_element_type=jnp.float32,
                )
                for j in range(step):
                    acc = acc + w[j0 + j] * jnp.maximum(logits[j * T : (j + 1) * T, :], 0.0)
            out_ref[:, s : s + tile] = acc


def score(q, w, k):
    return pl.pallas_call(
        score_kernel,
        in_specs=[IN_HBM, IN_VMEM, IN_HBM],
        out_specs=[IN_VMEM] * 2,
        out_shape=[f32(T, S), jax.ShapeDtypeStruct((ROWS, D), jnp.bfloat16)],
        scratch_shapes=[
            pltpu.VMEM((2, T, JL // 2, D), jnp.bfloat16),
            pltpu.VMEM((S, D), jnp.bfloat16),
            pltpu.VMEM((HALF, D), jnp.float32),
            pltpu.SemaphoreType.DMA((3,)),
        ],
        compiler_params=params(SCORE_VMEM),
        name="score",
    )(q, w, k)


def valid_mask(ctx):
    key = ctx * S + lax.broadcasted_iota(jnp.int32, (T, S), 1)
    query = POS + lax.broadcasted_iota(jnp.int32, (T, S), 0)
    return key <= query


def target_kernel(who_ref, target_ref, index_ref, w_ref, q_ref, normal_ref, sums_ref, held_ref, weighted_ref, payload_ref):
    held_ref[...] = index_ref[...]
    w = columns_of([w_ref[j : j + 1, :] for j in range(JL)])
    for j in range(JL):
        at = slice(j * T, (j + 1) * T)
        weighted_ref[at, :] = (q_ref[at, :].astype(jnp.float32) * w[j]).astype(jnp.bfloat16)
    core = who_ref[1]
    payload_ref[:HALF, :] = q_ref[pl.ds(pl.multiple_of(core * HALF, HALF), HALF), :].astype(jnp.float32)
    part = w_ref[pl.ds(pl.multiple_of(core * N_NEAR, N_NEAR), N_NEAR), :]
    payload_ref[HALF:, :] = jnp.concatenate([part, jnp.zeros((N_NEAR, 128 - T), jnp.float32)], axis=1)
    valid = valid_mask(who_ref[0])
    target = target_ref[...]
    masked = jnp.where(valid, target, 0.0)
    mass = jnp.sum(masked, axis=1, keepdims=True)
    entropy = jnp.sum(masked * jnp.log(target), axis=1, keepdims=True)
    normal_ref[...] = masked * (1.0 / mass)
    lane = lax.broadcasted_iota(jnp.int32, (T, 128), 1)
    sums_ref[...] = jnp.where(lane == 0, mass, entropy)


def target_sums(who, target, partial_index, w, q):
    return pl.pallas_call(
        target_kernel,
        in_specs=[IN_SMEM] + [IN_VMEM] * 4,
        out_specs=[IN_VMEM] * 5,
        out_shape=[
            f32(T, S),
            f32(T, 128),
            f32(T, S),
            jax.ShapeDtypeStruct((ROWS, D), jnp.bfloat16),
            f32(HALF + N_NEAR, D),
        ],
        compiler_params=params(),
        name="target",
    )(who, target, partial_index, w, q)


def stats_kernel(who_ref, mine_ref, other_ref, target_ref, sums_ref, index_ref, stats_ref, parts_ref):
    index = mine_ref[...] + other_ref[...]
    index_ref[...] = index
    valid = valid_mask(who_ref[0])
    target = target_ref[...]
    row_max = jnp.max(jnp.where(valid, index, -jnp.inf), axis=1, keepdims=True)
    expo = jnp.where(valid, jnp.exp(index - row_max), 0.0)
    denom = jnp.sum(expo, axis=1, keepdims=True)
    mass, entropy = sums_ref[:, 0:1], sums_ref[:, 1:2]
    cross = mass * jnp.sum(target * index, axis=1, keepdims=True)
    lane = lax.broadcasted_iota(jnp.int32, (T, 128), 1)
    packed = jnp.zeros((T, 128), jnp.float32)
    soft = expo * (1.0 / denom)
    peaks = (jnp.sum(x * x, axis=1, keepdims=True) for x in (soft, target))
    mixed = jnp.where(next(peaks) <= 4.0 * next(peaks), 1.0, 0.0)
    for i, column in enumerate((row_max, denom, mass, entropy, cross, mixed)):
        packed = jnp.where(lane == i, column, packed)
    packed = jnp.concatenate([packed, jnp.zeros((128 - T, 128), jnp.float32)], axis=0)
    stats_ref[...] = jnp.transpose(packed)[:8, :]
    parts_ref[0] = soft.astype(jnp.bfloat16)
    parts_ref[1] = (mixed * soft - target).astype(jnp.bfloat16)


def local_stats(who, mine, other, target, sums):
    return pl.pallas_call(
        stats_kernel,
        in_specs=[IN_SMEM] + [IN_VMEM] * 4,
        out_specs=[IN_VMEM] * 3,
        out_shape=[f32(T, S), f32(8, 128), jax.ShapeDtypeStruct((2, T, S), jnp.bfloat16)],
        compiler_params=params(),
        name="stats",
    )(who, mine, other, target, sums)


def query_kernel(who_ref, parts_ref, stats_ref, q_ref, k_ref, out_ref):
    block = 4 * T
    for r in range(0, HALF, block):
        at = pl.multiple_of(who_ref[0] * HALF + r, block)
        logits = lax.dot_general(
            q_ref[pl.ds(at, block), :], k_ref[...], NT, preferred_element_type=jnp.float32
        )
        positive = logits.astype(jnp.bfloat16) > 0.0
        for i in range(2):
            part = jnp.concatenate([parts_ref[i]] * (block // T), axis=0)
            picked = jnp.where(positive, part, jnp.zeros_like(part))
            at = slice(i * HALF + r, i * HALF + r + block)
            out_ref[at, :] = jnp.dot(picked, k_ref[...], preferred_element_type=jnp.float32)
    out_ref[ROWS:, :] = stats_ref[...]


def query_sums(half, parts, stats, q, k, name):
    return pl.pallas_call(
        query_kernel,
        in_specs=[IN_SMEM] + [IN_VMEM] * 4,
        out_specs=IN_VMEM,
        out_shape=f32(ROWS + 8, D),
        compiler_params=params(),
        cost_estimate=cost(6 * HALF * S * D, 4 << 20),
        name=name,
    )(half, parts, stats, q, k)


def merge(stats):
    row_max = stats[0][0:1]
    for s in stats[1:]:
        row_max = jnp.maximum(row_max, s[0:1])
    denom, rest = 0.0, 0.0
    for s in stats:
        denom = denom + s[1:2] * jnp.exp(s[0:1] - row_max)
        rest = rest + s[2:8]
    return jnp.concatenate([row_max, denom, rest], axis=0)


def shares(part, total):
    return part[1:2] * jnp.exp(part[0:1] - total[0:1]) / total[1:2], part[2:3] / total[2:3]


def pack_kernel(keep_ref, recv_ref, out_ref):
    mine, other = keep_ref[ROWS:, :], recv_ref[ROWS:, :]
    chip = merge([mine, other])
    rows = [*shares(mine, chip), mine[5:6], *shares(other, chip), other[5:6]]
    soft_a, target_a, mixed_a, soft_b, target_b, mixed_b = columns_of(rows)
    gap_a, gap_b = soft_a - mixed_a * target_a, soft_b - mixed_b * target_b
    for i in range(N_NEAR):
        at, too = slice(i * CHUNK, (i + 1) * CHUNK), slice(HALF + i * CHUNK, HALF + (i + 1) * CHUNK)
        a, b = keep_ref[at, :], recv_ref[at, :]
        out_ref[i, :CHUNK, :] = soft_a * a + soft_b * b
        gap = gap_a * a + gap_b * b + target_a * keep_ref[too, :] + target_b * recv_ref[too, :]
        out_ref[i, CHUNK : 2 * CHUNK, :] = gap
        out_ref[i, 2 * CHUNK :, :] = chip


def pack(keep, recv):
    return pl.pallas_call(
        pack_kernel,
        in_specs=[IN_VMEM] * 2,
        out_specs=IN_VMEM,
        out_shape=f32(N_NEAR, 2 * CHUNK + 8, 128),
        compiler_params=params(),
        name="pack",
    )(keep, recv)


def combine_parts(refs):
    parts = [ref[2 * CHUNK :, :] for ref in refs]
    total = merge(parts)
    columns = columns_of([row for part in parts for row in shares(part, total)])
    soft_sum, gap_sum = 0.0, 0.0
    for i, ref in enumerate(refs):
        soft, target = columns[2 * i], columns[2 * i + 1]
        a = ref[:CHUNK, :]
        soft_sum = soft_sum + soft * a
        gap_sum = gap_sum + (soft - target) * a + target * ref[CHUNK : 2 * CHUNK, :]
    return total, soft_sum, gap_sum


def near_kernel(in_ref, out_ref):
    total, soft_sum, gap_sum = combine_parts([in_ref.at[i] for i in range(N_NEAR)])
    out_ref[:CHUNK, :] = soft_sum
    out_ref[CHUNK : 2 * CHUNK, :] = gap_sum
    out_ref[2 * CHUNK :, :] = total


def combine_near(received):
    return pl.pallas_call(
        near_kernel,
        in_specs=[IN_VMEM],
        out_specs=IN_VMEM,
        out_shape=f32(2 * CHUNK + 8, D),
        compiler_params=params(),
        name="combine_near",
    )(received)


def far_kernel(who_ref, a_ref, b_ref, c_ref, d_ref, w_ref, q_ref, out_ref, stats_ref, loss_ref):
    total, _, gap_sum = combine_parts([a_ref, b_ref, c_ref, d_ref])
    row_max, denom, mass, entropy, cross = (total[i : i + 1] for i in range(5))
    stats_ref[...] = total
    loss = entropy / mass - jnp.log(mass) - cross / mass + row_max + jnp.log(denom)
    loss_ref[...] = loss[0, :T]
    gap_sum = gap_sum * (SCALE / T)
    head = who_ref[2]
    scaled = gap_sum * columns_of([w_ref[pl.ds(head, 1), :]])[0]
    q = q_ref[pl.ds(pl.multiple_of(head * T, T), T), :].astype(jnp.float32)
    grads = jnp.broadcast_to(jnp.sum(gap_sum * q, axis=1, keepdims=True), (T, 128))
    grads = jnp.transpose(jnp.concatenate([grads, grads], axis=0))[:8]
    for p in range(N_NEAR):
        out_ref[p, :CHUNK, :] = scaled
        out_ref[p, CHUNK:, :] = grads


def combine_far(who, own, far, w, q):
    return pl.pallas_call(
        far_kernel,
        in_specs=[IN_SMEM] + [IN_VMEM] * 6,
        out_specs=[IN_VMEM] * 3,
        out_shape=[f32(N_NEAR, CHUNK + 8, D), f32(8, 128), f32(T)],
        compiler_params=params(),
        name="combine_far",
    )(who, own, *far, w, q)


def place_half(half, at, out_hbm, sem):
    copies = []
    for p in range(N_NEAR):
        ref, i = at(p)
        to = out_hbm.at[:, half * N_NEAR + p, :]
        copies.append(pltpu.make_async_copy(ref.at[i, :CHUNK, :], to, sem.at[p]))
    for copy in copies:
        copy.start()
    return copies


def first_kernel(who_ref, mine_ref, out_hbm, sem):
    for copy in place_half(who_ref[1], lambda p: (mine_ref, p), out_hbm, sem):
        copy.wait()


def last_kernel(who_ref, mine_ref, other_ref, begun_hbm, out_hbm, weights_hbm, sem, weights_ref, weights_sem):
    def mine_at(p):
        return mine_ref, p

    def other_at(p):
        return other_ref, p

    copies = place_half(1 - who_ref[1], other_at, out_hbm, sem)

    def emit(first, second):
        for half, at in enumerate((first, second)):
            for p in range(N_NEAR):
                ref, i = at(p)
                row = half * N_NEAR + p
                weights_ref[row : row + 1, :] = ref[i, CHUNK : CHUNK + 1, :T]

    pl.when(who_ref[1] == 0)(lambda: emit(mine_at, other_at))
    pl.when(who_ref[1] == 1)(lambda: emit(other_at, mine_at))
    copies.append(pltpu.make_async_copy(weights_ref, weights_hbm, weights_sem))
    copies[-1].start()
    for copy in copies:
        copy.wait()


HALF_SCRATCH = [pltpu.SemaphoreType.DMA((N_NEAR,))]


def place_mine(who, mine):
    return pl.pallas_call(
        first_kernel,
        in_specs=[IN_SMEM, IN_VMEM],
        out_specs=IN_HBM,
        out_shape=f32(T, JL, D),
        scratch_shapes=HALF_SCRATCH,
        compiler_params=params(),
        name="place_mine",
    )(who, mine)


def place_other(who, mine, other, begun):
    return pl.pallas_call(
        last_kernel,
        in_specs=[IN_SMEM, IN_VMEM, IN_VMEM, IN_HBM],
        out_specs=[IN_HBM] * 2,
        out_shape=[f32(T, JL, D), f32(JL, T)],
        scratch_shapes=HALF_SCRATCH + [pltpu.VMEM((JL, T), jnp.float32), pltpu.SemaphoreType.DMA(())],
        input_output_aliases={3: 0},
        compiler_params=params(),
        name="place_other",
    )(who, mine, *other, begun)


def unpack_kernel(payload_ref, q_ref, weighted_ref):
    w = columns_of([payload_ref[HALF + j : HALF + j + 1, :] for j in range(N_NEAR)])
    for j in range(N_NEAR):
        at = slice(j * T, (j + 1) * T)
        q = payload_ref[at, :]
        q_ref[at, :] = q.astype(jnp.bfloat16)
        weighted_ref[at, :] = (q * w[j]).astype(jnp.bfloat16)


KEY_TILE = 256


def key_sums(gap, k, q_ref, weighted_ref):
    span = 1024
    gap = jnp.concatenate([gap] * (span // 128), axis=1)
    acc = jnp.zeros((KEY_TILE, D), jnp.float32)
    for r in range(0, q_ref.shape[0], span):
        logits = lax.dot_general(k, q_ref[r : r + span, :], NT, preferred_element_type=jnp.float32)
        picked = jnp.where(logits > 0.0, gap, 0.0).astype(jnp.bfloat16)
        acc = acc + jnp.dot(picked, weighted_ref[r : r + span, :], preferred_element_type=jnp.float32)
    return acc


def own_kernel(who_ref, index_ref, target_ref, stats_ref, q_ref, weighted_ref, k_ref, out_ref, gap_ref):
    row_max, denom, mass = columns_of([stats_ref[i : i + 1, :] for i in range(3)])
    gap = jnp.exp(index_ref[...] - row_max) * (1.0 / denom) - target_ref[...] * (1.0 / mass)
    gap = jnp.where(valid_mask(who_ref[0]), gap, 0.0) * (SCALE / T)
    for s in range(0, S, KEY_TILE):
        at = slice(s, s + KEY_TILE)
        turned = jnp.transpose(jnp.concatenate([gap[:, at]] * 2, axis=0))
        gap_ref[at, :] = turned
        out_ref[at, :] = key_sums(turned, k_ref[at, :], q_ref, weighted_ref)


def own_key_grads(who, index, target, stats, q, weighted, k):
    return pl.pallas_call(
        own_kernel,
        in_specs=[IN_SMEM] + [IN_VMEM] * 6,
        out_specs=[IN_VMEM] * 2,
        out_shape=[f32(S, D)] * 2,
        compiler_params=params(),
        cost_estimate=cost(4 * ROWS * S * D, 4 << 20),
        name="own_key_grads",
    )(who, index, target, stats, q, weighted, k)


def other_kernel(
    own_ref, gap_ref, k_ref, payload_a_ref, payload_b_ref, out_hbm,
    q_a_ref, weighted_a_ref, q_b_ref, weighted_b_ref, out_ref, sems,
):
    unpack_kernel(payload_a_ref, q_a_ref, weighted_a_ref)
    unpack_kernel(payload_b_ref, q_b_ref, weighted_b_ref)
    copies = []
    for s in range(0, S, KEY_TILE):
        at = slice(s, s + KEY_TILE)
        gap, k = gap_ref[at, :], k_ref[at, :]
        both = key_sums(gap, k, q_a_ref, weighted_a_ref) + key_sums(gap, k, q_b_ref, weighted_b_ref)
        out_ref[at, :] = own_ref[at, :] + both
        copies.append(pltpu.make_async_copy(out_ref.at[at], out_hbm.at[at], sems.at[s // KEY_TILE]))
        copies[-1].start()
    for copy in copies:
        copy.wait()


def key_grads(own, gap, k, *heads):
    return pl.pallas_call(
        other_kernel,
        in_specs=[IN_VMEM] * 5,
        out_specs=IN_HBM,
        out_shape=f32(S, D),
        scratch_shapes=[pltpu.VMEM((HALF, D), jnp.bfloat16)] * 4
        + [pltpu.VMEM((S, D), jnp.float32), pltpu.SemaphoreType.DMA((S // KEY_TILE,))],
        compiler_params=params(),
        cost_estimate=cost(4 * ROWS * S * D, 4 << 20),
        name="key_grads",
    )(own, gap, k, *heads)


def on_device(index_queries, head_weights, index_keys, main_target):
    swap = [(0, 1), (1, 0)]
    core = lax.axis_index("c")
    head = core * N_NEAR + lax.axis_index(NEAR)
    who = jnp.stack([lax.axis_index(CTX), core, head]).astype(jnp.int32)
    w = head_weights.T
    partial_index, q = score(index_queries, w, index_keys)
    other_index = lax.ppermute(partial_index, "yh", swap)
    target, target_sum, held_index, weighted, payload = target_sums(who, main_target, partial_index, w, q)
    payload = lax.ppermute(payload, "yh", swap)
    payloads = [payload, lax.ppermute(payload, "c", swap)]
    index, stats, parts = local_stats(who, held_index, other_index, target, target_sum)

    send = query_sums(1 - who[1:2], parts, stats, q, index_keys, "query_sums_send")
    recv = lax.ppermute(send, "c", swap)
    keep = query_sums(who[1:2], parts, stats, q, index_keys, "query_sums_keep")
    near = lax.all_to_all(pack(keep, recv), NEAR, 0, 0, tiled=True)
    own = combine_near(near)
    far = [lax.ppermute(own, FAR, [(i, i ^ d) for i in range(N_FAR)]) for d in range(1, N_FAR)]
    chunk, total_stats, loss = combine_far(who, own, far, w, q)

    mine = lax.all_to_all(chunk, NEAR, 0, 0, tiled=True)
    own, gap = own_key_grads(who, index, main_target, total_stats, q, weighted, index_keys)
    grad_keys = key_grads(own, gap, index_keys, *payloads)
    mine, grad_keys = lax.optimization_barrier((mine, grad_keys))
    other = [lax.ppermute(mine, "c", swap)]
    grad_queries, grad_weights = place_other(who, mine, other, place_mine(who, mine))
    return grad_queries, grad_weights.T, grad_keys, loss


def solution(mesh):
    fine = Mesh(mesh.devices.reshape(N_FAR, 2, 2, 4, 2, 2), CTX + ("yh",))
    return jax.shard_map(
        on_device,
        mesh=fine,
        in_specs=(P(None, "yh", None), P(None, "yh"), P(CTX, None), P(None, CTX)),
        out_specs=(P(None, "yh", None), P(None, "yh"), P(CTX, None), P()),
        check_vma=False,
    )
```
